128 devices in a mesh: gx: 16 (over z, x), gy: 8 (over y, core).
Axes of the slice: x: 4, y: 4, z: 4, core: 2. Of those that a mesh axis runs over, the one named last changes fastest.
Arguments:
- sea_temp: float32 [2048, 4096], P('gy', 'gx'), may hold values from -1.9 to 1.5
- air_cooling: float32 [2048, 4096], P('gy', 'gx'), may hold values from 0.2 to 2
- ocean_current: float32 [2, 2048, 4096], P(None, 'gy', 'gx'), may hold values from -3 to 3
- wind_stress: float32 [2, 2048, 4096], P(None, 'gy', 'gx'), may hold values from -3 to 3
- land_mask: int32 [2048, 4096], P('gy', 'gx'), may hold values 0 or 1
- velocity: float32 [2, 2048, 4096], P(None, 'gy', 'gx'), may hold values from -2 to 2
- stress: float32 [3, 2048, 4096], P(None, 'gy', 'gx'), may hold values from -3 to 3
- block_owner: int32 [8, 256], P('gy', 'gx'), may hold values from 0 to 15, as said below
- ice_thick: float32 [5, 8, 512, 4096], P(None, 'gy', 'gx'), may hold values from 0.1 to 4
- ice_area: float32 [5, 8, 512, 4096], P(None, 'gy', 'gx'), may hold values from 0.02 to 0.2
- ice_present: int32 [5, 8, 512, 4096], P(None, 'gy', 'gx'), may hold values 0 or 1
Outputs:
- new_thick: float32 [5, 8, 512, 4096], P(None, 'gy', 'gx')
- surface_flux: float32 [2, 2048, 4096], P(None, 'gy', 'gx')
- velocity_out: float32 [2, 2048, 4096], P(None, 'gy', 'gx')
- stress_out: float32 [3, 2048, 4096], P(None, 'gy', 'gx')
The draws below stay inside these ranges and needn't reach their ends.
Inputs may be any that keep to these rules, and one draw needn't show every extreme that they name: `block_owner`: each entry names an owner in the same gy row; no device names one owner for more than 2 of its blocks.
All inputs are finite; a program needn't handle non-finite values. No bound on the sum of `land_mask` or of `ice_present` on one device may be relied on, other than what follows from the above.
Results may differ from the reference program's by a relative error of at most 0.00012.
Values sent between devices are 32-bit elements; how exact they have to be, the bound alone decides.
A program may use at most 128 MiB of HBM per device.

```python
import math
import jax
import jax.numpy as jnp
from jax import lax

CX = 256
BROWS = 16
NBLK = 16
CAP = 2
NCAT = 5
NSUB = 8
NY = 2048
NX = 4096
SLOTS = 32
BCELLS = 4096
N_GX = 16
N_GY = 8


def draw_block_owner(key, part):
    key = jax.random.fold_in(key, 11)
    subkeys = jax.random.split(key, 4)
    busiest = jax.random.randint(subkeys[0], (N_GY, 1, 1), 0, N_GX)
    scores = jax.random.randint(subkeys[1], (N_GY, N_GX, N_GX - 1), 0, 1 << 20) * 64 + jnp.arange(N_GX - 1)
    ranking = jnp.argsort(scores, axis=-1).astype(jnp.int32)
    pattern = jax.random.randint(subkeys[2], (N_GY, N_GX, 1), 0, 2)
    positions = jnp.arange(NBLK - CAP)
    chosen = jnp.where(pattern == 0, positions % (N_GX - 1), positions // 2)
    chosen = jnp.broadcast_to(chosen, (N_GY, N_GX, NBLK - CAP)).astype(jnp.int32)
    picked = jnp.take_along_axis(ranking, chosen, axis=-1)
    others = picked + (picked >= busiest).astype(jnp.int32)
    owners = jnp.concatenate([jnp.broadcast_to(busiest, (N_GY, N_GX, CAP)), others], -1)
    mixing = jax.random.randint(subkeys[3], (N_GY, N_GX, NBLK), 0, 1 << 20) * 64 + jnp.arange(NBLK)
    shuffle = jnp.argsort(mixing, axis=-1).astype(jnp.int32)
    owners = jnp.take_along_axis(owners, shuffle, axis=-1)
    return owners.reshape(N_GY, N_GX * NBLK).astype(jnp.int32)


def place_ends(result, own_key, least, largest):
    shape = result.shape
    index_at = [jax.random.randint(jax.random.fold_in(own_key, axis), (), 0, shape[axis]) for axis in range(len(shape))]
    result = result.at[tuple(index_at)].set(least)
    longest = shape.index(max(shape))
    index_at[longest] = (index_at[longest] + 1) % shape[longest]
    return result.at[tuple(index_at)].set(largest)


def block_levels(rng, dims, shards, low, high):
    gain = 1.0
    for dim, parts in shards:
        steps = jax.random.uniform(jax.random.fold_in(jax.random.fold_in(rng, 6), dim), (parts,), jnp.float32, low / len(shards), high / len(shards))
        gain = gain * jnp.repeat(jnp.exp(steps), dims[dim] // parts).reshape((-1,) + (1,) * (len(dims) - 1 - dim))
    return gain


def gaussian(key, dims, deviation, most, pieces=(), held_as=jnp.bfloat16):
    values = jax.random.normal(key, dims, jnp.float32) * deviation
    if len(pieces) > 0:
        values = block_levels(key, dims, pieces, -0.22, 0.18) * values
    return jnp.clip(values, min=-most, max=most).astype(held_as)


def setup_inputs(seed: int = 0) -> dict:
    keys = jax.random.split(jax.random.key(seed), 12)
    sea_temp = jnp.clip(-1.9 + 3.4 * jax.random.uniform(keys[0], (NY, NX), jnp.float32) ** block_levels(keys[0], (NY, NX), ((0, 8), (1, 16)), -0.2, 0.2), -1.9, 1.5)
    air_cooling = jnp.clip(jnp.exp(math.log(2.0) - 2.3025851 * jax.random.uniform(keys[1], (NY, NX), jnp.float32) ** block_levels(keys[1], (NY, NX), ((0, 8), (1, 16)), -0.2, 0.2)), 0.2, 2.0)
    ocean_current = gaussian(keys[2], (2, NY, NX), 0.5, 3.0, ((1, 8), (2, 16)), jnp.float32)
    wind_stress = gaussian(keys[3], (2, NY, NX), 0.5, 3.0, ((1, 8), (2, 16)), jnp.float32)
    land_mask = place_ends((jax.random.randint(keys[4], (NY, NX), 0, 8) < 1).astype(jnp.int32), jax.random.fold_in(keys[4], 1), 0, 1)
    velocity = gaussian(keys[5], (2, NY, NX), 0.3, 2.0, ((1, 8), (2, 16)), jnp.float32)
    stress = gaussian(keys[6], (3, NY, NX), 0.5, 3.0, ((1, 8), (2, 16)), jnp.float32)
    block_owner = draw_block_owner(jax.random.fold_in(keys[11], 71), 0)
    ice_thick = jnp.clip(jnp.exp(math.log(4.0) - 3.6888794 * jax.random.uniform(keys[8], (NCAT, N_GY, N_GX * SLOTS, BCELLS), jnp.float32) ** block_levels(keys[8], (NCAT, N_GY, N_GX * SLOTS, BCELLS), ((1, 8), (2, 16)), -0.2, 0.2)), 0.1, 4.0)
    ice_area = jnp.clip(0.02 + 0.18 * jax.random.uniform(keys[9], (NCAT, N_GY, N_GX * SLOTS, BCELLS), jnp.float32) ** block_levels(keys[9], (NCAT, N_GY, N_GX * SLOTS, BCELLS), ((1, 8), (2, 16)), -0.2, 0.2), 0.02, 0.2)
    ice_present = place_ends((jax.random.randint(keys[10], (NCAT, N_GY, N_GX * SLOTS, BCELLS), 0, 4) < 3).astype(jnp.int32), jax.random.fold_in(keys[10], 1), 0, 1)
    return dict(sea_temp=sea_temp, air_cooling=air_cooling, ocean_current=ocean_current, wind_stress=wind_stress, land_mask=land_mask, velocity=velocity, stress=stress, block_owner=block_owner, ice_thick=ice_thick, ice_area=ice_area, ice_present=ice_present)


HIGHEST = lax.Precision.HIGHEST

def grow_ice(routed_temp, routed_cool, thick_live, area_live):
    basal_flux = 0.5 * (routed_temp + 1.8)
    change = 0.4 * (routed_cool * 0.5 / (thick_live + 0.5) - basal_flux)
    grown = jnp.maximum(thick_live + change, 0.0)
    ice_cover = lax.optimization_barrier(jnp.sum(area_live, 0))
    ice_mass = lax.optimization_barrier(jnp.sum(area_live * grown, 0))
    heat_flux = ice_cover * basal_flux - (1.0 - ice_cover) * routed_cool
    fresh_flux = -lax.optimization_barrier(jnp.sum(area_live * change, 0))
    return (grown, heat_flux, fresh_flux, ice_mass, ice_cover)

def strain_rates(zonal_pad, merid_pad):
    zonal_east = (zonal_pad[1:-1, 2:] - zonal_pad[1:-1, :-2]) * 0.5
    merid_north = (merid_pad[2:, 1:-1] - merid_pad[:-2, 1:-1]) * 0.5
    zonal_north = (zonal_pad[2:, 1:-1] - zonal_pad[:-2, 1:-1]) * 0.5
    merid_east = (merid_pad[1:-1, 2:] - merid_pad[1:-1, :-2]) * 0.5
    return (zonal_east + merid_north, zonal_east - merid_north, zonal_north + merid_east)

def relax_stress(stresses, divergence, tension, shearing, strength):
    deform = jnp.sqrt(divergence * divergence + (tension * tension + shearing * shearing) / 4.0 + 0.04)
    factor = strength / deform
    new_sum = (stresses[0] + 0.5 * (factor * divergence - strength)) / 1.5
    new_diff = (stresses[1] + 0.5 * factor * tension / 4.0) / 1.5
    new_shear = (stresses[2] + 0.5 * factor * shearing / 4.0) / 1.5
    return jnp.stack([new_sum, new_diff, new_shear])

def move_ice(velocity, stress_pad, wind_stress, ocean_current, inertia, wet_cells):
    along_x = 0.5 * (stress_pad[0] + stress_pad[1])
    along_y = 0.5 * (stress_pad[0] - stress_pad[1])
    shear_pad = stress_pad[2]
    force_east = 0.5 * (along_x[1:-1, 2:] - along_x[1:-1, :-2]) + 0.5 * (shear_pad[2:, 1:-1] - shear_pad[:-2, 1:-1])
    force_north = 0.5 * (shear_pad[1:-1, 2:] - shear_pad[1:-1, :-2]) + 0.5 * (along_y[2:, 1:-1] - along_y[:-2, 1:-1])
    forces = jnp.stack([force_east, force_north])
    return wet_cells * (velocity + 0.3 / inertia * (forces + wind_stress + 0.8 * ocean_current)) / (1.0 + 0.3 * 0.8 / inertia)

def reference(sea_temp, air_cooling, ocean_current, wind_stress, land_mask, velocity, stress, block_owner, ice_thick, ice_area, ice_present):
    owner_table = block_owner.reshape(N_GY, N_GX, NBLK)
    same_owner = owner_table[..., :, None] == owner_table[..., None, :]
    earlier = jnp.arange(NBLK)[None, :] < jnp.arange(NBLK)[:, None]
    block_rank = lax.optimization_barrier(jnp.sum((same_owner & earlier).astype(jnp.int32), -1)).astype(jnp.int32)
    target = owner_table * CAP + block_rank
    select = (jnp.arange(SLOTS)[:, None] == target[..., None, :]).astype(jnp.float32)

    def to_blocks(values):
        return values.reshape(N_GY, NBLK, BROWS, N_GX, CX).transpose(0, 3, 1, 2, 4).reshape(N_GY, N_GX, NBLK, BCELLS)

    def route(values):
        routed = jnp.einsum('rstb,rsbc->rstc', select, to_blocks(values), precision=HIGHEST)
        return routed.reshape(N_GY, N_GX, N_GX, CAP, BCELLS).transpose(0, 2, 1, 3, 4).reshape(N_GY, N_GX * SLOTS, BCELLS)

    def unroute(values):
        returned = values.reshape(N_GY, N_GX, N_GX, CAP, BCELLS).transpose(0, 2, 1, 3, 4).reshape(N_GY, N_GX, SLOTS, BCELLS)
        blocks = jnp.einsum('rstb,rstc->rsbc', select, returned, precision=HIGHEST)
        return blocks.reshape(N_GY, N_GX, NBLK, BROWS, CX).transpose(0, 2, 3, 1, 4).reshape(NY, NX)
    present = ice_present.astype(jnp.float32)
    thick_live = ice_thick * present
    area_live = ice_area * present
    grown, heat_flux, fresh_flux, ice_mass, ice_cover = grow_ice(route(sea_temp), route(air_cooling), thick_live, area_live)
    counts = lax.optimization_barrier(jnp.sum((owner_table[..., None] == jnp.arange(N_GX)).astype(jnp.int32), 2))
    filled = (counts.transpose(0, 2, 1)[..., None] > jnp.arange(CAP)).reshape(N_GY, N_GX * SLOTS, 1).astype(jnp.float32)
    new_thick = filled[None] * present * grown
    heat_grid = unroute(heat_flux)
    fresh_grid = unroute(fresh_flux)
    mass_grid = unroute(ice_mass)
    cover_grid = unroute(ice_cover)
    strength = mass_grid * jnp.exp(-2.0 * (1.0 - cover_grid))
    inertia = mass_grid + 0.5
    wet_cells = 1.0 - land_mask.astype(jnp.float32)
    padding = ((0, 0), (1, 1), (1, 1))
    for subcycle in range(NSUB):
        vel_pad = jnp.pad(velocity, padding)
        divergence, tension, shearing = strain_rates(vel_pad[0], vel_pad[1])
        stress = relax_stress(stress, divergence, tension, shearing, strength)
        velocity = move_ice(velocity, jnp.pad(stress, padding), wind_stress, ocean_current, inertia, wet_cells)
    return (new_thick, jnp.stack([heat_grid, fresh_grid]), velocity, stress)
```

```python
import functools

import jax
import jax.numpy as jnp
from jax import lax
from jax.experimental import pallas as pl
from jax.experimental.pallas import tpu as pltpu
from jax.sharding import PartitionSpec as P

F32 = jnp.float32
MESH = pl.DeviceIdType.MESH
NSUB = 8
NCAT = 5
NBLK = 16
STEPS = (
    (0, 1), (0, 3), (1, 0), (3, 0), (1, 1), (3, 3), (1, 3), (3, 1),
    (2, 2), (0, 2), (2, 0), (1, 2), (2, 1), (3, 2), (2, 3),
)
ROWS = 304
OWN = 24
NO_BLOCK = 1.0e6
U, V, X, Y, H, FU, FV, WET = range(8)


def kernel(
    owner_ref, sea_hbm, air_hbm, cur_hbm, wind_hbm, land_hbm, vel_hbm, str_hbm, thick_hbm, area_hbm, pres_hbm,
    nt_hbm, flux_hbm, velo_hbm, stro_hbm,
    sea, air, thick, area, pres, rc, nt, wind, cur, land,
    snd, rcv, scov, smass, ss1, rcov, rmass, rs1, got,
    S, M, PL, PR, QL, QR, ML, MR, NL, NR, KL, KR, flux,
    cA, cB, cG, cK, outb,
    lsem, osem, snd_s, snd_r, cov_s, cov_r, mass_s, mass_r, s1_s, s1_r, hs, hr, ms, mr,
):
    r = lax.axis_index("gy")
    s = lax.axis_index("gx")
    z, x = s // 4, s % 4

    def dev(dz, dx):
        return ((z + dz) % 4) * 4 + (x + dx) % 4

    loads = {}

    def load(name, src, dst):
        c = pltpu.make_async_copy(src, dst, lsem.at[len(loads)])
        c.start()
        loads[name] = c

    load("sea", sea_hbm, sea)
    load("air", air_hbm, air)
    load("thick", thick_hbm, thick)
    load("area", area_hbm, area)
    load("pres", pres_hbm, pres)
    for t in range(2):
        lanes = pl.ds(t * 128, 128)
        load(("vel", t), vel_hbm.at[:, :, lanes], S.at[pl.ds(U, 2), t, pl.ds(OWN, 256)])
        load(("str", t), str_hbm.at[:, :, lanes], S.at[pl.ds(X, 3), t, pl.ds(OWN, 256)])
        load(("wind", t), wind_hbm.at[:, :, lanes], wind.at[:, t])
        load(("cur", t), cur_hbm.at[:, :, lanes], cur.at[:, t])
        load(("land", t), land_hbm.at[:, lanes], land.at[t])

    barrier = pltpu.get_barrier_semaphore()
    north, south = (r + 1) % 8, (r + 7) % 8
    east, west = (s + 1) % 16, (s + 15) % 16
    for dz, dx in STEPS:
        pl.semaphore_signal(barrier, inc=1, device_id={"gx": dev(dz, dx)}, device_id_type=MESH)
    for ry in (north, south):
        for sx in (west, s, east):
            pl.semaphore_signal(barrier, inc=1, device_id={"gy": ry, "gx": sx}, device_id_type=MESH)

    owners = [owner_ref[0, b] for b in range(NBLK)]
    spare = jnp.zeros((8, 128), F32)
    for f in range(5):
        for t in range(3):
            S[f, t, pl.ds(0, 8), :] = spare
            S[f, t, pl.ds(ROWS - 8, 8), :] = spare

    loads["sea"].wait()
    loads["air"].wait()
    pl.semaphore_wait(barrier, 21)

    def stage(buf, row0, target):
        hits = [(owners[b] == target).astype(jnp.int32) for b in range(NBLK)]
        count = hits[0]
        first = last = hits[0] * 0
        for b in range(1, NBLK):
            first = first + hits[b] * (1 - jnp.minimum(count, 1)) * b
            last = last + hits[b] * (b - last)
            count = count + hits[b]
        for k, b in ((0, first), (1, last)):
            filled = (count > k).astype(jnp.int32).astype(F32)
            temp_b = sea[b] * filled + NO_BLOCK * (1.0 - filled)
            cool_b = air[b]
            for half in range(2):
                at = row0 + k * 64 + half * 16
                buf[pl.ds(at, 16), :] = temp_b[:, half * 128 : half * 128 + 128]
                buf[pl.ds(at + 32, 16), :] = cool_b[:, half * 128 : half * 128 + 128]

    sends = []
    for i, (dz, dx) in enumerate(STEPS):
        target = dev(dz, dx)
        stage(snd, i * 128, target)
        c = pltpu.make_async_remote_copy(
            src_ref=snd.at[pl.ds(i * 128, 128)], dst_ref=rcv.at[pl.ds(pl.multiple_of(s * 128, 128), 128)],
            send_sem=snd_s.at[i], recv_sem=snd_r.at[i], device_id={"gx": target}, device_id_type=MESH,
        )
        c.start()
        sends.append(c)
    stage(rcv, pl.multiple_of(s * 128, 128), s)

    for n in ("thick", "area", "pres"):
        loads[n].wait()

    def prepare(g, row, half):
        lanes = pl.ds(pl.multiple_of(row * 256 + half * 128, 128), 128)
        slots = pl.ds(pl.multiple_of(g * 8, 8), 8)
        cover = jnp.zeros((8, 128), F32)
        s1 = jnp.zeros((8, 128), F32)
        for c in range(NCAT):
            p = pres[c, slots, lanes].astype(F32)
            tl = thick[c, slots, lanes] * p
            al = area[c, slots, lanes] * p
            inv = 1.0 / (tl + 0.5)
            thick[c, slots, lanes] = tl
            area[c, slots, lanes] = al
            rc[c, slots, lanes] = inv
            cover = cover + al
            s1 = s1 + al * inv
        at = g * 256 + half * 16 + row
        scov[pl.ds(at, 8, stride=32), :] = cover
        ss1[pl.ds(at, 8, stride=32), :] = s1

    @pl.loop(0, 64)
    def _(i):
        for half in range(2):
            prepare(i // 16, i % 16, half)

    def back(buf, dst, ssem, rsem, i):
        dz, dx = STEPS[i]
        target = dev(-dz, -dx)
        return pltpu.make_async_remote_copy(
            src_ref=buf.at[pl.ds(pl.multiple_of(target * 64, 64), 64)],
            dst_ref=dst.at[pl.ds(pl.multiple_of(s * 64, 64), 64)],
            send_sem=ssem.at[i], recv_sem=rsem.at[i], device_id={"gx": target}, device_id_type=MESH,
        )

    covs = [back(scov, rcov, cov_s, cov_r, i) for i in range(15)]
    for c in covs:
        c.start()
    mine = pl.ds(pl.multiple_of(s * 64, 64), 64)
    rcov[mine, :] = scov[mine, :]
    rs1[mine, :] = ss1[mine, :]

    for t in range(2):
        for n in ("vel", "str", "wind", "cur", "land"):
            loads[(n, t)].wait()

    lane = lax.broadcasted_iota(jnp.int32, (8, 128), 1)
    own_rows = lambda i: pl.ds(pl.multiple_of(OWN + i * 8, 8), 8)

    @pl.loop(0, 32)
    def _(i):
        at = own_rows(i)
        raw = pl.ds(pl.multiple_of(i * 8, 8), 8)
        fields = []
        for t in range(2):
            total, diff = S[X, t, at, :], S[Y, t, at, :]
            S[X, t, at, :] = total + diff
            S[Y, t, at, :] = total - diff
            S[H, t, at, :] = 2.0 * S[H, t, at, :]
            S[FU, t, at, :] = wind[0, t, raw, :] + 0.8 * cur[0, t, raw, :]
            S[FV, t, at, :] = wind[1, t, raw, :] + 0.8 * cur[1, t, raw, :]
            S[WET, t, at, :] = 1.0 - land[t, raw, :].astype(F32)
        left = S[0, 0, at, :]
        right = pltpu.roll(S[0, 1, at, :], 16, 1)
        for f in range(1, 8):
            here = (lane >= 16 * f) & (lane < 16 * f + 16)
            left = jnp.where(here, pltpu.roll(S[f, 0, at, :], 16 * f, 1), left)
            last = S[f, 1, at, :]
            right = jnp.where(here, pltpu.roll(last, 16 * f + 16, 1) if f < 7 else last, right)
        PL[raw, :] = left
        PR[raw, :] = right

    first16, last16 = pl.ds(OWN, 16), pl.ds(OWN + 240, 16)
    above, below = pl.ds(280, 16), pl.ds(8, 16)

    def remote(src, dst, sems, n, to):
        return pltpu.make_async_remote_copy(
            src_ref=src, dst_ref=dst, send_sem=sems[0].at[n], recv_sem=sems[1].at[n],
            device_id=to, device_id_type=MESH,
        )

    two = pl.ds(0, 2)
    sems = (hs, hr)
    halo = [
        remote(PL, QR.at[pl.ds(16, 256)], sems, 0, {"gx": west}),
        remote(PR, QL.at[pl.ds(16, 256)], sems, 1, {"gx": east}),
        remote(S.at[:, two, first16], S.at[:, two, above], sems, 2, {"gy": south}),
        remote(S.at[:, two, last16], S.at[:, two, below], sems, 3, {"gy": north}),
        remote(PL.at[pl.ds(0, 16)], QR.at[pl.ds(272, 16)], sems, 4, {"gy": south, "gx": west}),
        remote(PR.at[pl.ds(0, 16)], QL.at[pl.ds(272, 16)], sems, 5, {"gy": south, "gx": east}),
        remote(PL.at[pl.ds(240, 16)], QR.at[pl.ds(0, 16)], sems, 6, {"gy": north, "gx": west}),
        remote(PR.at[pl.ds(240, 16)], QL.at[pl.ds(0, 16)], sems, 7, {"gy": north, "gx": east}),
    ]
    for c in halo:
        c.start()

    stores = []
    masses = [back(smass, rmass, mass_s, mass_r, i) for i in range(15)]

    for dz in range(4):
        group = (z + 4 - dz) % 4
        for i in range(15):
            if STEPS[i][0] == dz:
                sends[i].wait_recv()

        def grow(row, half):
            lanes = pl.ds(pl.multiple_of(row * 256 + half * 128, 128), 128)
            slots = pl.ds(pl.multiple_of(group * 8, 8), 8)
            at = group * 512 + half * 16 + row
            heat_in = 0.2 * (rcv[pl.ds(at, 8, stride=64), :] + 1.8)
            cool_in = 0.2 * rcv[pl.ds(at + 32, 8, stride=64), :]
            mass = jnp.zeros((8, 128), F32)
            for c in range(NCAT):
                change = cool_in * rc[c, slots, lanes] - heat_in
                grown = jnp.maximum(thick[c, slots, lanes] + change, 0.0)
                mass = mass + area[c, slots, lanes] * grown
                nt[c, slots, lanes] = pres[c, slots, lanes].astype(F32) * grown
            smass[pl.ds(group * 256 + half * 16 + row, 8, stride=32), :] = mass

        @pl.loop(0, 16)
        def _(row):
            for half in range(2):
                grow(row, half)

        for i in range(15):
            if STEPS[i][0] == dz:
                masses[i].start()
        slots = pl.ds(pl.multiple_of(group * 8, 8), 8)
        c = pltpu.make_async_copy(nt.at[:, slots], nt_hbm.at[:, slots], osem.at[dz])
        c.start()
        stores.append(c)
    rmass[mine, :] = smass[mine, :]
    s1s = [back(ss1, rs1, s1_s, s1_r, i) for i in range(15)]

    at_west, at_east = s == 0, s == 15
    at_south, at_north = r == 0, r == 7
    for c in halo:
        c.wait_recv()

    def beside(right, left, shift_right, shift_left):
        a = jnp.where(at_east, 0.0, pltpu.roll(right, shift_right, 1) if shift_right else right)
        b = jnp.where(at_west, 0.0, pltpu.roll(left, shift_left, 1) if shift_left else left)
        return jnp.where(lane < 16, a, jnp.where(lane >= 112, b, 0.0))

    @pl.loop(0, 36)
    def _(i):
        raw = pl.ds(pl.multiple_of(i * 8, 8), 8)
        at = pl.ds(pl.multiple_of(i * 8 + 8, 8), 8)
        right, left = QR[raw, :], QL[raw, :]
        for f in range(8):
            S[f, 2, at, :] = beside(right, left, (128 - 16 * f) % 128, (112 - 16 * f) % 128)

    def clear_outside(ref, n):
        for at, gone in ((below, at_south), (above, at_north)):
            for f in range(n):
                for t in range(3):
                    ref[f, t, at, :] = jnp.where(gone, 0.0, ref[f, t, at, :])

    clear_outside(S, 8)

    slot_of = []
    for b in range(NBLK):
        slot = owners[b] * 2
        for e in range(b):
            slot = slot + (owners[e] == owners[b]).astype(jnp.int32)
        slot_of.append(slot)
    for c in covs:
        c.wait_recv()
    for c in masses:
        c.wait_recv()
    for k in range(32):
        got[0, k] = rmass[pl.ds(k * 32, 32), :]
        got[1, k] = rcov[pl.ds(k * 32, 32), :]
    for b in range(NBLK):
        mass, cover = got[0, slot_of[b]], got[1, slot_of[b]]
        strength = mass * jnp.exp(-2.0 * (1.0 - cover))
        temp_b, cool_b = sea[b], air[b]
        for half in range(2):
            part = slice(half * 16, half * 16 + 16)
            lanes = slice(half * 128, half * 128 + 128)
            M[0, half, pl.ds(OWN + b * 16, 16), :] = mass[part]
            M[1, half, pl.ds(OWN + b * 16, 16), :] = strength[part]
            cv = cover[part]
            flux[0, half, pl.ds(b * 16, 16), :] = cv * (0.5 * (temp_b[:, lanes] + 1.8)) - (1.0 - cv) * cool_b[:, lanes]

    for i in range(8):
        left = jnp.zeros((8, 128), F32)
        right = left
        for chunk in range(4):
            for f in range(2):
                at = pl.ds(OWN + chunk * 64 + i * 8, 8)
                k = 32 * chunk + 16 * f
                here = (lane >= k) & (lane < k + 16)
                a, b = M[f, 0, at, :], M[f, 1, at, :]
                left = jnp.where(here, pltpu.roll(a, k, 1) if k else a, left)
                right = jnp.where(here, pltpu.roll(b, (k + 16) % 128, 1) if k != 112 else b, right)
        ML[pl.ds(i * 8, 8), :] = left
        MR[pl.ds(i * 8, 8), :] = right
    sems = (ms, mr)
    halo_m = [
        remote(ML, NR, sems, 0, {"gx": west}),
        remote(MR, NL, sems, 1, {"gx": east}),
        remote(M.at[:, two, first16], M.at[:, two, above], sems, 2, {"gy": south}),
        remote(M.at[:, two, last16], M.at[:, two, below], sems, 3, {"gy": north}),
        remote(ML.at[pl.ds(0, 16)], KR.at[1], sems, 4, {"gy": south, "gx": west}),
        remote(MR.at[pl.ds(0, 16)], KL.at[1], sems, 5, {"gy": south, "gx": east}),
        remote(ML.at[pl.ds(48, 16)], KR.at[0], sems, 6, {"gy": north, "gx": west}),
        remote(MR.at[pl.ds(48, 16)], KL.at[0], sems, 7, {"gy": north, "gx": east}),
    ]
    for c in halo_m:
        c.start()
    for c in s1s:
        c.start()
    for c in halo_m:
        c.wait_recv()
    for f in range(2):
        for chunk in range(4):
            k = 32 * chunk + 16 * f
            for i in range(8):
                at = pl.ds(OWN + chunk * 64 + i * 8, 8)
                raw = pl.ds(i * 8, 8)
                M[f, 2, at, :] = beside(NR[raw, :], NL[raw, :], (128 - k) % 128, (112 - k) % 128)
        for i in range(2):
            raw = pl.ds(i * 8, 8)
            k = 96 + 16 * f
            M[f, 2, pl.ds(8 + i * 8, 8), :] = beside(KR[0, raw, :], KL[0, raw, :], 128 - k, (112 - k) % 128)
            k = 16 * f
            M[f, 2, pl.ds(280 + i * 8, 8), :] = beside(KR[1, raw, :], KL[1, raw, :], (128 - k) % 128, 112 - k)
    clear_outside(M, 2)

    @pl.loop(1, 37)
    def _(i):
        at = pl.ds(pl.multiple_of(i * 8, 8), 8)
        for t in range(3):
            inertia = M[0, t, at, :] + 0.5
            w = S[WET, t, at, :] / (inertia + 0.24)
            cA[t, at, :] = w * inertia
            cB[t, at, :] = 0.075 * w
            cG[0, t, at, :] = 0.3 * w * S[FU, t, at, :]
            cG[1, t, at, :] = 0.3 * w * S[FV, t, at, :]
            cK[t, at, :] = M[1, t, at, :] * (1.0 / 6.0)

    for c in halo:
        c.wait_send()
    R = 8
    wide = lax.broadcasted_iota(jnp.int32, (R, 128), 1)
    is_last, is_first = wide == 127, wide == 0

    def across(f, at):
        v = [S[f, t, at, :] for t in range(3)]
        up = [pltpu.roll(a, 127, 1) for a in v]
        down = [pltpu.roll(a, 1, 1) for a in v]
        return [
            jnp.where(is_last, up[(t + 1) % 3], up[t]) - jnp.where(is_first, down[(t + 2) % 3], down[t])
            for t in range(3)
        ]

    def along(f, t, row0):
        return S[f, t, pl.ds(row0 + 1, R), :] - S[f, t, pl.ds(row0 - 1, R), :]

    @pl.loop(0, NSUB)
    def _(n):
        @pl.loop(0, 288 // R)
        def _(i):
            row0 = pl.multiple_of(i * R + 8, 8)
            at = pl.ds(row0, R)
            ux, vx = across(U, at), across(V, at)
            for t in range(3):
                a, b = ux[t], along(V, t, row0)
                sh = along(U, t, row0) + vx[t]
                d, e = a + b, a - b
                k = cK[t, at, :]
                d4 = 4.0 * d
                q = d * d4 + e * e + (sh * sh + 0.64)
                f = k * lax.rsqrt(q)
                k2 = k + k
                S[X, t, at, :] = S[X, t, at, :] * (1.0 / 1.5) + (f * (d4 + e) - k2)
                S[Y, t, at, :] = S[Y, t, at, :] * (1.0 / 1.5) + (f * (d4 - e) - k2)
                S[H, t, at, :] = S[H, t, at, :] * (1.0 / 1.5) + (f + f) * sh

        @pl.loop(0, 288 // R)
        def _(i):
            row0 = pl.multiple_of(i * R + 8, 8)
            at = pl.ds(row0, R)
            xx, hx = across(X, at), across(H, at)
            for t in range(3):
                a, b = cA[t, at, :], cB[t, at, :]
                fe = xx[t] + along(H, t, row0)
                fn = hx[t] + along(Y, t, row0)
                S[U, t, at, :] = a * S[U, t, at, :] + (b * fe + cG[0, t, at, :])
                S[V, t, at, :] = a * S[V, t, at, :] + (b * fn + cG[1, t, at, :])

    @pl.loop(0, 32)
    def _(i):
        at = own_rows(i)
        raw = pl.ds(pl.multiple_of(i * 8, 8), 8)
        for t in range(2):
            a, b = S[X, t, at, :], S[Y, t, at, :]
            outb[0, t, raw, :] = 0.5 * (a + b)
            outb[1, t, raw, :] = 0.5 * (a - b)
            outb[2, t, raw, :] = 0.5 * S[H, t, at, :]

    def store(src, dst):
        c = pltpu.make_async_copy(src, dst, osem.at[len(stores)])
        c.start()
        stores.append(c)

    for t in range(2):
        lanes = pl.ds(t * 128, 128)
        store(S.at[pl.ds(U, 2), t, pl.ds(OWN, 256)], velo_hbm.at[:, :, lanes])
        store(outb.at[:, t], stro_hbm.at[:, :, lanes])

    for c in s1s:
        c.wait_recv()
    for k in range(32):
        got[2, k] = rs1[pl.ds(k * 32, 32), :]
    for b in range(NBLK):
        s1, cover = got[2, slot_of[b]], got[1, slot_of[b]]
        temp_b, cool_b = sea[b], air[b]
        for half in range(2):
            part = slice(half * 16, half * 16 + 16)
            lanes = slice(half * 128, half * 128 + 128)
            basal = 0.5 * (temp_b[:, lanes] + 1.8)
            flux[1, half, pl.ds(b * 16, 16), :] = 0.4 * (basal * cover[part] - 0.5 * cool_b[:, lanes] * s1[part])
    for t in range(2):
        store(flux.at[:, t], flux_hbm.at[:, :, pl.ds(t * 128, 128)])
    for c in sends + covs + masses + s1s + halo_m:
        c.wait_send()
    for c in stores:
        c.wait()


def local(sea, air, cur, wind, land, vel, stress, owner, thick, area, pres):
    any_ = pl.BlockSpec(memory_space=pl.ANY)
    vm = lambda *shape, dtype=F32: pltpu.VMEM(shape, dtype)
    dma = lambda n: pltpu.SemaphoreType.DMA((n,))
    nt, flux, velo, stro = pl.pallas_call(
        kernel,
        out_shape=(
            jax.ShapeDtypeStruct((NCAT, 32, 4096), F32),
            jax.ShapeDtypeStruct((2, 256, 256), F32),
            jax.ShapeDtypeStruct((2, 256, 256), F32),
            jax.ShapeDtypeStruct((3, 256, 256), F32),
        ),
        in_specs=[pl.BlockSpec(memory_space=pltpu.SMEM)] + [any_] * 10,
        out_specs=(any_,) * 4,
        scratch_shapes=[
            vm(16, 16, 256), vm(16, 16, 256),
            vm(NCAT, 32, 4096), vm(NCAT, 32, 4096), vm(NCAT, 32, 4096, dtype=jnp.int32),
            vm(NCAT, 32, 4096), vm(NCAT, 32, 4096),
            vm(2, 2, 256, 128), vm(2, 2, 256, 128), vm(2, 256, 128, dtype=jnp.int32),
            vm(15 * 128, 128), vm(16 * 128, 128),
            vm(1024, 128), vm(1024, 128), vm(1024, 128),
            vm(1024, 128), vm(1024, 128), vm(1024, 128), vm(3, 32, 32, 128),
            vm(8, 3, ROWS, 128), vm(2, 3, ROWS, 128),
            vm(256, 128), vm(256, 128), vm(288, 128), vm(288, 128),
            vm(64, 128), vm(64, 128), vm(64, 128), vm(64, 128), vm(2, 16, 128), vm(2, 16, 128),
            vm(2, 2, 256, 128),
            vm(3, ROWS, 128), vm(3, ROWS, 128), vm(2, 3, ROWS, 128), vm(3, ROWS, 128),
            vm(3, 2, 256, 128),
            dma(15), dma(10),
            dma(15), dma(15), dma(15), dma(15), dma(15), dma(15), dma(15), dma(15),
            dma(8), dma(8), dma(8), dma(8),
        ],
        compiler_params=pltpu.CompilerParams(
            collective_id=0, has_side_effects=True, vmem_limit_bytes=48 * 1024 * 1024
        ),
    )(
        owner, sea.reshape(16, 16, 256), air.reshape(16, 16, 256), cur, wind, land, vel, stress,
        thick.reshape(NCAT, 32, 4096), area.reshape(NCAT, 32, 4096), pres.reshape(NCAT, 32, 4096),
    )
    return nt.reshape(NCAT, 1, 32, 4096), flux, velo, stro


def solution(mesh):
    grid, pair, ice = P("gy", "gx"), P(None, "gy", "gx"), P(None, "gy", "gx", None)
    return jax.shard_map(
        local,
        mesh=mesh,
        in_specs=(grid, grid, pair, pair, grid, pair, pair, grid, ice, ice, ice),
        out_specs=(ice, pair, pair, pair),
        check_vma=False,
    )
```

```python
import functools

import jax
import jax.numpy as jnp
from jax import lax
from jax.experimental import pallas as pl
from jax.experimental.pallas import tpu as pltpu
from jax.sharding import PartitionSpec as P

F32 = jnp.float32
MESH = pl.DeviceIdType.MESH
NSUB = 8
NCAT = 5
NBLK = 16
STEPS = (
    (1, 2), (0, 2), (2, 1), (2, 0), (3, 2), (0, 1), (2, 3), (1, 0),
    (2, 2), (0, 3), (1, 1), (3, 0), (3, 3), (1, 3), (3, 1),
)
ROWS = 304
OWN = 24
NO_BLOCK = 1.0e6
U, V, X, Y, H, FU, FV, WET = range(8)


def kernel(
    owner_ref, sea_hbm, air_hbm, cur_hbm, wind_hbm, land_hbm, vel_hbm, str_hbm, thick_hbm, area_hbm, pres_hbm,
    nt_hbm, flux_hbm, velo_hbm, stro_hbm,
    sea, air, thick, area, pres, rc, nt, wind, cur, land,
    snd, rcv, scov, smass, ss1, rcov, rmass, rs1, got,
    S, M, PL, PR, QL, QR, ML, MR, NL, NR, KL, KR, flux,
    cA, cB, cG, cK, outb,
    lsem, osem, snd_s, snd_r, cov_s, cov_r, mass_s, mass_r, s1_s, s1_r, hs, hr, ms, mr,
):
    r = lax.axis_index("gy")
    s = lax.axis_index("gx")
    z, x = s // 4, s % 4

    odd = r % 2

    def dev(dz, dx):
        dz, dx = dz + odd * (dx - dz), dx + odd * (dz - dx)
        return ((z + dz) % 4) * 4 + (x + dx) % 4

    loads = {}

    def load(name, src, dst):
        c = pltpu.make_async_copy(src, dst, lsem.at[len(loads)])
        c.start()
        loads[name] = c

    load("sea", sea_hbm, sea)
    load("air", air_hbm, air)
    load("thick", thick_hbm, thick)
    load("area", area_hbm, area)
    load("pres", pres_hbm, pres)
    for t in range(2):
        lanes = pl.ds(t * 128, 128)
        load(("vel", t), vel_hbm.at[:, :, lanes], S.at[pl.ds(U, 2), t, pl.ds(OWN, 256)])
        load(("str", t), str_hbm.at[:, :, lanes], S.at[pl.ds(X, 3), t, pl.ds(OWN, 256)])
        load(("wind", t), wind_hbm.at[:, :, lanes], wind.at[:, t])
        load(("cur", t), cur_hbm.at[:, :, lanes], cur.at[:, t])
        load(("land", t), land_hbm.at[:, lanes], land.at[t])

    barrier = pltpu.get_barrier_semaphore()
    north, south = (r + 1) % 8, (r + 7) % 8
    east, west = (s + 1) % 16, (s + 15) % 16
    for dz, dx in STEPS:
        pl.semaphore_signal(barrier, inc=1, device_id={"gx": dev(dz, dx)}, device_id_type=MESH)
    for ry in (north, south):
        for sx in (west, s, east):
            pl.semaphore_signal(barrier, inc=1, device_id={"gy": ry, "gx": sx}, device_id_type=MESH)

    owners = [owner_ref[0, b] for b in range(NBLK)]
    spare = jnp.zeros((8, 128), F32)
    for f in range(5):
        for t in range(3):
            S[f, t, pl.ds(0, 8), :] = spare
            S[f, t, pl.ds(ROWS - 8, 8), :] = spare

    loads["sea"].wait()
    loads["air"].wait()

    def stage(buf, row0, target):
        hits = [(owners[b] == target).astype(jnp.int32) for b in range(NBLK)]
        count = hits[0]
        first = last = hits[0] * 0
        for b in range(1, NBLK):
            first = first + hits[b] * (1 - jnp.minimum(count, 1)) * b
            last = last + hits[b] * (b - last)
            count = count + hits[b]
        for k, b in ((0, first), (1, last)):
            filled = (count > k).astype(jnp.int32).astype(F32)
            temp_b = sea[b] * filled + NO_BLOCK * (1.0 - filled)
            cool_b = air[b]
            for half in range(2):
                at = row0 + k * 64 + half * 16
                buf[pl.ds(at, 16), :] = temp_b[:, half * 128 : half * 128 + 128]
                buf[pl.ds(at + 32, 16), :] = cool_b[:, half * 128 : half * 128 + 128]

    for i, (dz, dx) in enumerate(STEPS):
        stage(snd, i * 128, dev(dz, dx))
    pl.semaphore_wait(barrier, 21)
    sends = []
    for i, (dz, dx) in enumerate(STEPS):
        target = dev(dz, dx)
        c = pltpu.make_async_remote_copy(
            src_ref=snd.at[pl.ds(i * 128, 128)], dst_ref=rcv.at[pl.ds(pl.multiple_of(s * 128, 128), 128)],
            send_sem=snd_s.at[i], recv_sem=snd_r.at[i], device_id={"gx": target}, device_id_type=MESH,
        )
        c.start()
        sends.append(c)
    stage(rcv, pl.multiple_of(s * 128, 128), s)

    for n in ("thick", "area", "pres"):
        loads[n].wait()

    def prepare(g, row, half):
        lanes = pl.ds(pl.multiple_of(row * 256 + half * 128, 128), 128)
        slots = pl.ds(pl.multiple_of(g * 8, 8), 8)
        cover = jnp.zeros((8, 128), F32)
        s1 = jnp.zeros((8, 128), F32)
        for c in range(NCAT):
            p = pres[c, slots, lanes].astype(F32)
            tl = thick[c, slots, lanes] * p
            al = area[c, slots, lanes] * p
            inv = 1.0 / (tl + 0.5)
            thick[c, slots, lanes] = tl
            area[c, slots, lanes] = al
            rc[c, slots, lanes] = inv
            cover = cover + al
            s1 = s1 + al * inv
        at = g * 256 + half * 16 + row
        scov[pl.ds(at, 8, stride=32), :] = cover
        ss1[pl.ds(at, 8, stride=32), :] = s1

    @pl.loop(0, 64)
    def _(i):
        for half in range(2):
            prepare(i // 16, i % 16, half)

    def back(buf, dst, ssem, rsem, i):
        dz, dx = STEPS[i]
        target = dev(-dz, -dx)
        return pltpu.make_async_remote_copy(
            src_ref=buf.at[pl.ds(pl.multiple_of(target * 64, 64), 64)],
            dst_ref=dst.at[pl.ds(pl.multiple_of(s * 64, 64), 64)],
            send_sem=ssem.at[i], recv_sem=rsem.at[i], device_id={"gx": target}, device_id_type=MESH,
        )

    covs = [back(scov, rcov, cov_s, cov_r, i) for i in range(15)]
    for c in covs:
        c.start()
    mine = pl.ds(pl.multiple_of(s * 64, 64), 64)
    rcov[mine, :] = scov[mine, :]
    rs1[mine, :] = ss1[mine, :]

    for t in range(2):
        for n in ("vel", "str", "wind", "cur", "land"):
            loads[(n, t)].wait()

    lane = lax.broadcasted_iota(jnp.int32, (8, 128), 1)
    own_rows = lambda i: pl.ds(pl.multiple_of(OWN + i * 8, 8), 8)

    @pl.loop(0, 32)
    def _(i):
        at = own_rows(i)
        raw = pl.ds(pl.multiple_of(i * 8, 8), 8)
        fields = []
        for t in range(2):
            total, diff = S[X, t, at, :], S[Y, t, at, :]
            S[X, t, at, :] = total + diff
            S[Y, t, at, :] = total - diff
            S[H, t, at, :] = 2.0 * S[H, t, at, :]
            S[FU, t, at, :] = wind[0, t, raw, :] + 0.8 * cur[0, t, raw, :]
            S[FV, t, at, :] = wind[1, t, raw, :] + 0.8 * cur[1, t, raw, :]
            S[WET, t, at, :] = 1.0 - land[t, raw, :].astype(F32)
        left = S[0, 0, at, :]
        right = pltpu.roll(S[0, 1, at, :], 16, 1)
        for f in range(1, 8):
            here = (lane >= 16 * f) & (lane < 16 * f + 16)
            left = jnp.where(here, pltpu.roll(S[f, 0, at, :], 16 * f, 1), left)
            last = S[f, 1, at, :]
            right = jnp.where(here, pltpu.roll(last, 16 * f + 16, 1) if f < 7 else last, right)
        PL[raw, :] = left
        PR[raw, :] = right

    first16, last16 = pl.ds(OWN, 16), pl.ds(OWN + 240, 16)
    above, below = pl.ds(280, 16), pl.ds(8, 16)

    def remote(src, dst, sems, n, to):
        return pltpu.make_async_remote_copy(
            src_ref=src, dst_ref=dst, send_sem=sems[0].at[n], recv_sem=sems[1].at[n],
            device_id=to, device_id_type=MESH,
        )

    two = pl.ds(0, 2)
    sems = (hs, hr)
    halo = [
        remote(PL, QR.at[pl.ds(16, 256)], sems, 0, {"gx": west}),
        remote(PR, QL.at[pl.ds(16, 256)], sems, 1, {"gx": east}),
        remote(S.at[:, two, first16], S.at[:, two, above], sems, 2, {"gy": south}),
        remote(S.at[:, two, last16], S.at[:, two, below], sems, 3, {"gy": north}),
        remote(PL.at[pl.ds(0, 16)], QR.at[pl.ds(272, 16)], sems, 4, {"gy": south, "gx": west}),
        remote(PR.at[pl.ds(0, 16)], QL.at[pl.ds(272, 16)], sems, 5, {"gy": south, "gx": east}),
        remote(PL.at[pl.ds(240, 16)], QR.at[pl.ds(0, 16)], sems, 6, {"gy": north, "gx": west}),
        remote(PR.at[pl.ds(240, 16)], QL.at[pl.ds(0, 16)], sems, 7, {"gy": north, "gx": east}),
    ]
    for c in halo:
        c.start()

    for c in sends:
        c.wait_recv()

    def grow(g, row, half):
        lanes = pl.ds(pl.multiple_of(row * 256 + half * 128, 128), 128)
        slots = pl.ds(pl.multiple_of(g * 8, 8), 8)
        at = g * 512 + half * 16 + row
        heat_in = 0.2 * (rcv[pl.ds(at, 8, stride=64), :] + 1.8)
        cool_in = 0.2 * rcv[pl.ds(at + 32, 8, stride=64), :]
        mass = jnp.zeros((8, 128), F32)
        for c in range(NCAT):
            change = cool_in * rc[c, slots, lanes] - heat_in
            grown = jnp.maximum(thick[c, slots, lanes] + change, 0.0)
            mass = mass + area[c, slots, lanes] * grown
            nt[c, slots, lanes] = pres[c, slots, lanes].astype(F32) * grown
        smass[pl.ds(g * 256 + half * 16 + row, 8, stride=32), :] = mass

    @pl.loop(0, 32)
    def _(i):
        for k in range(2):
            for half in range(2):
                grow(i // 8, (i % 8) * 2 + k, half)

    masses = [back(smass, rmass, mass_s, mass_r, i) for i in range(15)]
    for c in masses:
        c.start()
    stores = []

    def store(src, dst):
        c = pltpu.make_async_copy(src, dst, osem.at[len(stores)])
        c.start()
        stores.append(c)

    store(nt, nt_hbm)
    rmass[mine, :] = smass[mine, :]
    s1s = [back(ss1, rs1, s1_s, s1_r, i) for i in range(15)]

    at_west, at_east = s == 0, s == 15
    at_south, at_north = r == 0, r == 7
    for c in halo:
        c.wait_recv()

    def beside(right, left, shift_right, shift_left):
        a = jnp.where(at_east, 0.0, pltpu.roll(right, shift_right, 1) if shift_right else right)
        b = jnp.where(at_west, 0.0, pltpu.roll(left, shift_left, 1) if shift_left else left)
        return jnp.where(lane < 16, a, jnp.where(lane >= 112, b, 0.0))

    @pl.loop(0, 36)
    def _(i):
        raw = pl.ds(pl.multiple_of(i * 8, 8), 8)
        at = pl.ds(pl.multiple_of(i * 8 + 8, 8), 8)
        right, left = QR[raw, :], QL[raw, :]
        for f in range(8):
            S[f, 2, at, :] = beside(right, left, (128 - 16 * f) % 128, (112 - 16 * f) % 128)

    def clear_outside(ref, n):
        for at, gone in ((below, at_south), (above, at_north)):
            for f in range(n):
                for t in range(3):
                    ref[f, t, at, :] = jnp.where(gone, 0.0, ref[f, t, at, :])

    clear_outside(S, 8)

    slot_of = []
    for b in range(NBLK):
        slot = owners[b] * 2
        for e in range(b):
            slot = slot + (owners[e] == owners[b]).astype(jnp.int32)
        slot_of.append(slot)
    for c in covs:
        c.wait_recv()
    for c in masses:
        c.wait_recv()
    for k in range(32):
        got[0, k] = rmass[pl.ds(k * 32, 32), :]
        got[1, k] = rcov[pl.ds(k * 32, 32), :]
    for b in range(NBLK):
        mass, cover = got[0, slot_of[b]], got[1, slot_of[b]]
        strength = mass * jnp.exp(-2.0 * (1.0 - cover))
        temp_b, cool_b = sea[b], air[b]
        for half in range(2):
            part = slice(half * 16, half * 16 + 16)
            lanes = slice(half * 128, half * 128 + 128)
            M[0, half, pl.ds(OWN + b * 16, 16), :] = mass[part]
            M[1, half, pl.ds(OWN + b * 16, 16), :] = strength[part]
            cv = cover[part]
            flux[0, half, pl.ds(b * 16, 16), :] = cv * (0.5 * (temp_b[:, lanes] + 1.8)) - (1.0 - cv) * cool_b[:, lanes]

    for i in range(8):
        left = jnp.zeros((8, 128), F32)
        right = left
        for chunk in range(4):
            for f in range(2):
                at = pl.ds(OWN + chunk * 64 + i * 8, 8)
                k = 32 * chunk + 16 * f
                here = (lane >= k) & (lane < k + 16)
                a, b = M[f, 0, at, :], M[f, 1, at, :]
                left = jnp.where(here, pltpu.roll(a, k, 1) if k else a, left)
                right = jnp.where(here, pltpu.roll(b, (k + 16) % 128, 1) if k != 112 else b, right)
        ML[pl.ds(i * 8, 8), :] = left
        MR[pl.ds(i * 8, 8), :] = right
    sems = (ms, mr)
    halo_m = [
        remote(ML, NR, sems, 0, {"gx": west}),
        remote(MR, NL, sems, 1, {"gx": east}),
        remote(M.at[:, two, first16], M.at[:, two, above], sems, 2, {"gy": south}),
        remote(M.at[:, two, last16], M.at[:, two, below], sems, 3, {"gy": north}),
        remote(ML.at[pl.ds(0, 16)], KR.at[1], sems, 4, {"gy": south, "gx": west}),
        remote(MR.at[pl.ds(0, 16)], KL.at[1], sems, 5, {"gy": south, "gx": east}),
        remote(ML.at[pl.ds(48, 16)], KR.at[0], sems, 6, {"gy": north, "gx": west}),
        remote(MR.at[pl.ds(48, 16)], KL.at[0], sems, 7, {"gy": north, "gx": east}),
    ]
    for c in halo_m:
        c.start()
    for c in s1s:
        c.start()
    for c in halo_m:
        c.wait_recv()
    for f in range(2):
        for chunk in range(4):
            k = 32 * chunk + 16 * f
            for i in range(8):
                at = pl.ds(OWN + chunk * 64 + i * 8, 8)
                raw = pl.ds(i * 8, 8)
                M[f, 2, at, :] = beside(NR[raw, :], NL[raw, :], (128 - k) % 128, (112 - k) % 128)
        for i in range(2):
            raw = pl.ds(i * 8, 8)
            k = 96 + 16 * f
            M[f, 2, pl.ds(8 + i * 8, 8), :] = beside(KR[0, raw, :], KL[0, raw, :], 128 - k, (112 - k) % 128)
            k = 16 * f
            M[f, 2, pl.ds(280 + i * 8, 8), :] = beside(KR[1, raw, :], KL[1, raw, :], (128 - k) % 128, 112 - k)
    clear_outside(M, 2)

    @pl.loop(1, 37)
    def _(i):
        at = pl.ds(pl.multiple_of(i * 8, 8), 8)
        for t in range(3):
            inertia = M[0, t, at, :] + 0.5
            w = S[WET, t, at, :] / (inertia + 0.24)
            cA[t, at, :] = w * inertia
            cB[t, at, :] = 0.075 * w
            cG[0, t, at, :] = 0.3 * w * S[FU, t, at, :]
            cG[1, t, at, :] = 0.3 * w * S[FV, t, at, :]
            cK[t, at, :] = M[1, t, at, :] * (1.0 / 6.0)

    for c in halo:
        c.wait_send()
    R = 288
    wide = lax.broadcasted_iota(jnp.int32, (R, 128), 1)
    is_last, is_first = wide == 127, wide == 0

    def across(f, at):
        v = [S[f, t, at, :] for t in range(3)]
        up = [pltpu.roll(a, 127, 1) for a in v]
        down = [pltpu.roll(a, 1, 1) for a in v]
        return [
            jnp.where(is_last, up[(t + 1) % 3], up[t]) - jnp.where(is_first, down[(t + 2) % 3], down[t])
            for t in range(3)
        ]

    def along(f, t, row0):
        return S[f, t, pl.ds(row0 + 1, R), :] - S[f, t, pl.ds(row0 - 1, R), :]

    @pl.loop(0, NSUB)
    def _(n):
        @pl.loop(0, 288 // R)
        def _(i):
            row0 = pl.multiple_of(i * R + 8, 8)
            at = pl.ds(row0, R)
            ux, vx = across(U, at), across(V, at)
            for t in range(3):
                a, b = ux[t], along(V, t, row0)
                sh = along(U, t, row0) + vx[t]
                d, e = a + b, a - b
                k = cK[t, at, :]
                d4 = 4.0 * d
                q = d * d4 + e * e + (sh * sh + 0.64)
                f = k * lax.rsqrt(q)
                k2 = k + k
                S[X, t, at, :] = S[X, t, at, :] * (1.0 / 1.5) + (f * (d4 + e) - k2)
                S[Y, t, at, :] = S[Y, t, at, :] * (1.0 / 1.5) + (f * (d4 - e) - k2)
                S[H, t, at, :] = S[H, t, at, :] * (1.0 / 1.5) + (f + f) * sh

        @pl.loop(0, 288 // R)
        def _(i):
            row0 = pl.multiple_of(i * R + 8, 8)
            at = pl.ds(row0, R)
            xx, hx = across(X, at), across(H, at)
            for t in range(3):
                a, b = cA[t, at, :], cB[t, at, :]
                fe = xx[t] + along(H, t, row0)
                fn = hx[t] + along(Y, t, row0)
                S[U, t, at, :] = a * S[U, t, at, :] + (b * fe + cG[0, t, at, :])
                S[V, t, at, :] = a * S[V, t, at, :] + (b * fn + cG[1, t, at, :])

    @pl.loop(0, 32)
    def _(i):
        at = own_rows(i)
        raw = pl.ds(pl.multiple_of(i * 8, 8), 8)
        for t in range(2):
            a, b = S[X, t, at, :], S[Y, t, at, :]
            outb[0, t, raw, :] = 0.5 * (a + b)
            outb[1, t, raw, :] = 0.5 * (a - b)
            outb[2, t, raw, :] = 0.5 * S[H, t, at, :]

    for t in range(2):
        lanes = pl.ds(t * 128, 128)
        store(S.at[pl.ds(U, 2), t, pl.ds(OWN, 256)], velo_hbm.at[:, :, lanes])
        store(outb.at[:, t], stro_hbm.at[:, :, lanes])

    for c in s1s:
        c.wait_recv()
    for k in range(32):
        got[2, k] = rs1[pl.ds(k * 32, 32), :]
    for b in range(NBLK):
        s1, cover = got[2, slot_of[b]], got[1, slot_of[b]]
        temp_b, cool_b = sea[b], air[b]
        for half in range(2):
            part = slice(half * 16, half * 16 + 16)
            lanes = slice(half * 128, half * 128 + 128)
            basal = 0.5 * (temp_b[:, lanes] + 1.8)
            flux[1, half, pl.ds(b * 16, 16), :] = 0.4 * (basal * cover[part] - 0.5 * cool_b[:, lanes] * s1[part])
    for t in range(2):
        store(flux.at[:, t], flux_hbm.at[:, :, pl.ds(t * 128, 128)])
    for c in sends + covs + masses + s1s + halo_m:
        c.wait_send()
    for c in stores:
        c.wait()


def hand_over(nt, flux, velo, stro, nt_out, flux_out, velo_out, stro_out, nt_v, flux_v, velo_v, stro_v, sem):
    parts = [(nt.at[c], nt_v.at[c], nt_out.at[c]) for c in range(NCAT)]
    parts += [(stro.at[c], stro_v.at[c], stro_out.at[c]) for c in range(3)]
    parts += [(velo.at[c], velo_v.at[c], velo_out.at[c]) for c in range(2)]
    parts += [(flux.at[c], flux_v.at[c], flux_out.at[c]) for c in range(2)]
    reads = [pltpu.make_async_copy(a, v, sem.at[0, i]) for i, (a, v, _) in enumerate(parts)]
    writes = [pltpu.make_async_copy(v, b, sem.at[1, i]) for i, (_, v, b) in enumerate(parts)]
    for c in reads:
        c.start()
    for c, d in zip(reads, writes):
        c.wait()
        d.start()
    for d in writes:
        d.wait()


def local(sea, air, cur, wind, land, vel, stress, owner, thick, area, pres):
    any_ = pl.BlockSpec(memory_space=pl.ANY)
    vm = lambda *shape, dtype=F32: pltpu.VMEM(shape, dtype)
    dma = lambda n: pltpu.SemaphoreType.DMA((n,))
    results = (
        jax.ShapeDtypeStruct((NCAT, 32, 4096), F32),
        jax.ShapeDtypeStruct((2, 256, 256), F32),
        jax.ShapeDtypeStruct((2, 256, 256), F32),
        jax.ShapeDtypeStruct((3, 256, 256), F32),
    )
    made = pl.pallas_call(
        kernel,
        out_shape=results,
        in_specs=[pl.BlockSpec(memory_space=pltpu.SMEM)] + [any_] * 10,
        out_specs=(any_,) * 4,
        scratch_shapes=[
            vm(16, 16, 256), vm(16, 16, 256),
            vm(NCAT, 32, 4096), vm(NCAT, 32, 4096), vm(NCAT, 32, 4096, dtype=jnp.int32),
            vm(NCAT, 32, 4096), vm(NCAT, 32, 4096),
            vm(2, 2, 256, 128), vm(2, 2, 256, 128), vm(2, 256, 128, dtype=jnp.int32),
            vm(15 * 128, 128), vm(16 * 128, 128),
            vm(1024, 128), vm(1024, 128), vm(1024, 128),
            vm(1024, 128), vm(1024, 128), vm(1024, 128), vm(3, 32, 32, 128),
            vm(8, 3, ROWS, 128), vm(2, 3, ROWS, 128),
            vm(256, 128), vm(256, 128), vm(288, 128), vm(288, 128),
            vm(64, 128), vm(64, 128), vm(64, 128), vm(64, 128), vm(2, 16, 128), vm(2, 16, 128),
            vm(2, 2, 256, 128),
            vm(3, ROWS, 128), vm(3, ROWS, 128), vm(2, 3, ROWS, 128), vm(3, ROWS, 128),
            vm(3, 2, 256, 128),
            dma(15), dma(10),
            dma(15), dma(15), dma(15), dma(15), dma(15), dma(15), dma(15), dma(15),
            dma(8), dma(8), dma(8), dma(8),
        ],
        compiler_params=pltpu.CompilerParams(
            collective_id=0, has_side_effects=True, vmem_limit_bytes=60 * 1024 * 1024
        ),
    )(
        owner, sea.reshape(16, 16, 256), air.reshape(16, 16, 256), cur, wind, land, vel, stress,
        thick.reshape(NCAT, 32, 4096), area.reshape(NCAT, 32, 4096), pres.reshape(NCAT, 32, 4096),
    )
    nt, flux, velo, stro = pl.pallas_call(
        hand_over,
        out_shape=results,
        in_specs=[any_] * 4,
        out_specs=(any_,) * 4,
        scratch_shapes=[vm(*o.shape) for o in results] + [pltpu.SemaphoreType.DMA((2, 12))],
        compiler_params=pltpu.CompilerParams(vmem_limit_bytes=60 * 1024 * 1024),
    )(*made)
    return nt.reshape(NCAT, 1, 32, 4096), flux, velo, stro


def solution(mesh):
    grid, pair, ice = P("gy", "gx"), P(None, "gy", "gx"), P(None, "gy", "gx", None)
    return jax.shard_map(
        local,
        mesh=mesh,
        in_specs=(grid, grid, pair, pair, grid, pair, pair, grid, ice, ice, ice),
        out_specs=(ice, pair, pair, pair),
        check_vma=False,
    )
```

```python
import functools

import jax
import jax.numpy as jnp
from jax import lax
from jax.experimental import pallas as pl
from jax.experimental.pallas import tpu as pltpu
from jax.sharding import PartitionSpec as P

F32 = jnp.float32
MESH = pl.DeviceIdType.MESH
NSUB = 8
NCAT = 5
NBLK = 16
STEPS = (
    (1, 2), (0, 2), (2, 1), (2, 0), (3, 2), (0, 1), (2, 3), (1, 0),
    (2, 2), (0, 3), (1, 1), (3, 0), (3, 3), (1, 3), (3, 1),
)
ROWS = 304
OWN = 24
NO_BLOCK = 1.0e6
U, V, X, Y, H, FU, FV, WET = range(8)


def kernel(
    owner_ref, sea_hbm, air_hbm, cur_hbm, wind_hbm, land_hbm, vel_hbm, str_hbm, thick_hbm, area_hbm, pres_hbm,
    nt_hbm, flux_hbm, velo_hbm, stro_hbm,
    sea, air, thick, area, pres, rc, nt, wind, cur, land,
    snd, rcv, scov, smass, ss1, rcov, rmass, rs1, got,
    S, M, PL, PR, QL, QR, ML, MR, NL, NR, KL, KR, flux,
    cA, cB, cG, cK, outb,
    lsem, osem, snd_s, snd_r, cov_s, cov_r, mass_s, mass_r, s1_s, s1_r, hs, hr, ms, mr,
):
    r = lax.axis_index("gy")
    s = lax.axis_index("gx")
    z, x = s // 4, s % 4

    odd = r % 2

    def dev(dz, dx):
        dz, dx = dz + odd * (dx - dz), dx + odd * (dz - dx)
        return ((z + dz) % 4) * 4 + (x + dx) % 4

    loads = {}

    def load(name, src, dst):
        c = pltpu.make_async_copy(src, dst, lsem.at[len(loads)])
        c.start()
        loads[name] = c

    load("sea", sea_hbm, sea)
    load("air", air_hbm, air)
    barrier = pltpu.get_barrier_semaphore()
    north, south = (r + 1) % 8, (r + 7) % 8
    east, west = (s + 1) % 16, (s + 15) % 16
    for dz, dx in STEPS:
        pl.semaphore_signal(barrier, inc=1, device_id={"gx": dev(dz, dx)}, device_id_type=MESH)
    for ry in (north, south):
        for sx in (west, s, east):
            pl.semaphore_signal(barrier, inc=1, device_id={"gy": ry, "gx": sx}, device_id_type=MESH)

    load("thick", thick_hbm, thick)
    load("area", area_hbm, area)
    load("pres", pres_hbm, pres)
    for t in range(2):
        lanes = pl.ds(t * 128, 128)
        load(("vel", t), vel_hbm.at[:, :, lanes], S.at[pl.ds(U, 2), t, pl.ds(OWN, 256)])
        load(("str", t), str_hbm.at[:, :, lanes], S.at[pl.ds(X, 3), t, pl.ds(OWN, 256)])
        load(("wind", t), wind_hbm.at[:, :, lanes], wind.at[:, t])
        load(("cur", t), cur_hbm.at[:, :, lanes], cur.at[:, t])
        load(("land", t), land_hbm.at[:, lanes], land.at[t])

    owners = [owner_ref[0, b] for b in range(NBLK)]
    spare = jnp.zeros((8, 128), F32)
    for f in range(5):
        for t in range(3):
            S[f, t, pl.ds(0, 8), :] = spare
            S[f, t, pl.ds(ROWS - 8, 8), :] = spare

    loads["sea"].wait()
    loads["air"].wait()

    def stage(buf, row0, target):
        hits = [(owners[b] == target).astype(jnp.int32) for b in range(NBLK)]
        count = hits[0]
        first = last = hits[0] * 0
        for b in range(1, NBLK):
            first = first + hits[b] * (1 - jnp.minimum(count, 1)) * b
            last = last + hits[b] * (b - last)
            count = count + hits[b]
        for k, b in ((0, first), (1, last)):
            filled = (count > k).astype(jnp.int32).astype(F32)
            temp_b = sea[b] * filled + NO_BLOCK * (1.0 - filled)
            cool_b = air[b]
            for half in range(2):
                at = row0 + k * 64 + half * 16
                buf[pl.ds(at, 16), :] = temp_b[:, half * 128 : half * 128 + 128]
                buf[pl.ds(at + 32, 16), :] = cool_b[:, half * 128 : half * 128 + 128]

    for i, (dz, dx) in enumerate(STEPS):
        stage(snd, i * 128, dev(dz, dx))
    pl.semaphore_wait(barrier, 21)
    sends = []
    for i, (dz, dx) in enumerate(STEPS):
        target = dev(dz, dx)
        c = pltpu.make_async_remote_copy(
            src_ref=snd.at[pl.ds(i * 128, 128)], dst_ref=rcv.at[pl.ds(pl.multiple_of(s * 128, 128), 128)],
            send_sem=snd_s.at[i], recv_sem=snd_r.at[i], device_id={"gx": target}, device_id_type=MESH,
        )
        c.start()
        sends.append(c)
    stage(rcv, pl.multiple_of(s * 128, 128), s)

    for n in ("thick", "area", "pres"):
        loads[n].wait()

    def prepare(g, row, half):
        lanes = pl.ds(pl.multiple_of(row * 256 + half * 128, 128), 128)
        slots = pl.ds(pl.multiple_of(g * 8, 8), 8)
        cover = jnp.zeros((8, 128), F32)
        s1 = jnp.zeros((8, 128), F32)
        for c in range(NCAT):
            p = pres[c, slots, lanes].astype(F32)
            tl = thick[c, slots, lanes] * p
            al = area[c, slots, lanes] * p
            inv = 1.0 / (tl + 0.5)
            thick[c, slots, lanes] = tl
            area[c, slots, lanes] = al
            rc[c, slots, lanes] = inv
            cover = cover + al
            s1 = s1 + al * inv
        at = g * 256 + half * 16 + row
        scov[pl.ds(at, 8, stride=32), :] = cover
        ss1[pl.ds(at, 8, stride=32), :] = s1

    @pl.loop(0, 64)
    def _(i):
        for half in range(2):
            prepare(i // 16, i % 16, half)

    def back(buf, dst, ssem, rsem, i):
        dz, dx = STEPS[i]
        target = dev(-dz, -dx)
        return pltpu.make_async_remote_copy(
            src_ref=buf.at[pl.ds(pl.multiple_of(target * 64, 64), 64)],
            dst_ref=dst.at[pl.ds(pl.multiple_of(s * 64, 64), 64)],
            send_sem=ssem.at[i], recv_sem=rsem.at[i], device_id={"gx": target}, device_id_type=MESH,
        )

    covs = [back(scov, rcov, cov_s, cov_r, i) for i in range(15)]
    for c in covs:
        c.start()
    mine = pl.ds(pl.multiple_of(s * 64, 64), 64)
    rcov[mine, :] = scov[mine, :]
    rs1[mine, :] = ss1[mine, :]

    for t in range(2):
        for n in ("vel", "str", "wind", "cur", "land"):
            loads[(n, t)].wait()

    lane = lax.broadcasted_iota(jnp.int32, (8, 128), 1)
    own_rows = lambda i: pl.ds(pl.multiple_of(OWN + i * 8, 8), 8)

    @pl.loop(0, 32)
    def _(i):
        at = own_rows(i)
        raw = pl.ds(pl.multiple_of(i * 8, 8), 8)
        fields = []
        for t in range(2):
            total, diff = S[X, t, at, :], S[Y, t, at, :]
            S[X, t, at, :] = total + diff
            S[Y, t, at, :] = total - diff
            S[H, t, at, :] = 2.0 * S[H, t, at, :]
            S[FU, t, at, :] = wind[0, t, raw, :] + 0.8 * cur[0, t, raw, :]
            S[FV, t, at, :] = wind[1, t, raw, :] + 0.8 * cur[1, t, raw, :]
            S[WET, t, at, :] = 1.0 - land[t, raw, :].astype(F32)
        left = S[0, 0, at, :]
        right = pltpu.roll(S[0, 1, at, :], 16, 1)
        for f in range(1, 8):
            here = (lane >= 16 * f) & (lane < 16 * f + 16)
            left = jnp.where(here, pltpu.roll(S[f, 0, at, :], 16 * f, 1), left)
            last = S[f, 1, at, :]
            right = jnp.where(here, pltpu.roll(last, 16 * f + 16, 1) if f < 7 else last, right)
        PL[raw, :] = left
        PR[raw, :] = right

    first16, last16 = pl.ds(OWN, 16), pl.ds(OWN + 240, 16)
    above, below = pl.ds(280, 16), pl.ds(8, 16)

    def remote(src, dst, sems, n, to):
        return pltpu.make_async_remote_copy(
            src_ref=src, dst_ref=dst, send_sem=sems[0].at[n], recv_sem=sems[1].at[n],
            device_id=to, device_id_type=MESH,
        )

    two = pl.ds(0, 2)
    sems = (hs, hr)
    halo = [
        remote(PL, QR.at[pl.ds(16, 256)], sems, 0, {"gx": west}),
        remote(PR, QL.at[pl.ds(16, 256)], sems, 1, {"gx": east}),
        remote(S.at[:, two, first16], S.at[:, two, above], sems, 2, {"gy": south}),
        remote(S.at[:, two, last16], S.at[:, two, below], sems, 3, {"gy": north}),
        remote(PL.at[pl.ds(0, 16)], QR.at[pl.ds(272, 16)], sems, 4, {"gy": south, "gx": west}),
        remote(PR.at[pl.ds(0, 16)], QL.at[pl.ds(272, 16)], sems, 5, {"gy": south, "gx": east}),
        remote(PL.at[pl.ds(240, 16)], QR.at[pl.ds(0, 16)], sems, 6, {"gy": north, "gx": west}),
        remote(PR.at[pl.ds(240, 16)], QL.at[pl.ds(0, 16)], sems, 7, {"gy": north, "gx": east}),
    ]
    for c in halo:
        c.start()

    for c in sends:
        c.wait_recv()

    def grow(g, row, half):
        lanes = pl.ds(pl.multiple_of(row * 256 + half * 128, 128), 128)
        slots = pl.ds(pl.multiple_of(g * 8, 8), 8)
        at = g * 512 + half * 16 + row
        heat_in = 0.2 * (rcv[pl.ds(at, 8, stride=64), :] + 1.8)
        cool_in = 0.2 * rcv[pl.ds(at + 32, 8, stride=64), :]
        mass = jnp.zeros((8, 128), F32)
        for c in range(NCAT):
            change = cool_in * rc[c, slots, lanes] - heat_in
            grown = jnp.maximum(thick[c, slots, lanes] + change, 0.0)
            mass = mass + area[c, slots, lanes] * grown
            nt[c, slots, lanes] = pres[c, slots, lanes].astype(F32) * grown
        smass[pl.ds(g * 256 + half * 16 + row, 8, stride=32), :] = mass

    @pl.loop(0, 32)
    def _(i):
        for k in range(2):
            for half in range(2):
                grow(i // 8, (i % 8) * 2 + k, half)

    masses = [back(smass, rmass, mass_s, mass_r, i) for i in range(15)]
    for c in masses:
        c.start()
    stores = []

    def store(src, dst):
        c = pltpu.make_async_copy(src, dst, osem.at[len(stores)])
        c.start()
        stores.append(c)

    store(nt, nt_hbm)
    rmass[mine, :] = smass[mine, :]
    s1s = [back(ss1, rs1, s1_s, s1_r, i) for i in range(15)]

    at_west, at_east = s == 0, s == 15
    at_south, at_north = r == 0, r == 7
    for c in halo:
        c.wait_recv()

    def beside(right, left, shift_right, shift_left):
        a = jnp.where(at_east, 0.0, pltpu.roll(right, shift_right, 1) if shift_right else right)
        b = jnp.where(at_west, 0.0, pltpu.roll(left, shift_left, 1) if shift_left else left)
        return jnp.where(lane < 16, a, jnp.where(lane >= 112, b, 0.0))

    @pl.loop(0, 36)
    def _(i):
        raw = pl.ds(pl.multiple_of(i * 8, 8), 8)
        at = pl.ds(pl.multiple_of(i * 8 + 8, 8), 8)
        right, left = QR[raw, :], QL[raw, :]
        for f in range(8):
            S[f, 2, at, :] = beside(right, left, (128 - 16 * f) % 128, (112 - 16 * f) % 128)

    def clear_outside(ref, n):
        for at, gone in ((below, at_south), (above, at_north)):
            for f in range(n):
                for t in range(3):
                    ref[f, t, at, :] = jnp.where(gone, 0.0, ref[f, t, at, :])

    clear_outside(S, 8)

    slot_of = []
    for b in range(NBLK):
        slot = owners[b] * 2
        for e in range(b):
            slot = slot + (owners[e] == owners[b]).astype(jnp.int32)
        slot_of.append(slot)
    for c in covs:
        c.wait_recv()
    for c in masses:
        c.wait_recv()
    for k in range(32):
        got[0, k] = rmass[pl.ds(k * 32, 32), :]
        got[1, k] = rcov[pl.ds(k * 32, 32), :]
    for b in range(NBLK):
        mass, cover = got[0, slot_of[b]], got[1, slot_of[b]]
        strength = mass * jnp.exp(-2.0 * (1.0 - cover))
        temp_b, cool_b = sea[b], air[b]
        for half in range(2):
            part = slice(half * 16, half * 16 + 16)
            lanes = slice(half * 128, half * 128 + 128)
            M[0, half, pl.ds(OWN + b * 16, 16), :] = mass[part]
            M[1, half, pl.ds(OWN + b * 16, 16), :] = strength[part]
            cv = cover[part]
            flux[0, half, pl.ds(b * 16, 16), :] = cv * (0.5 * (temp_b[:, lanes] + 1.8)) - (1.0 - cv) * cool_b[:, lanes]

    for i in range(8):
        left = jnp.zeros((8, 128), F32)
        right = left
        for chunk in range(4):
            for f in range(2):
                at = pl.ds(OWN + chunk * 64 + i * 8, 8)
                k = 32 * chunk + 16 * f
                here = (lane >= k) & (lane < k + 16)
                a, b = M[f, 0, at, :], M[f, 1, at, :]
                left = jnp.where(here, pltpu.roll(a, k, 1) if k else a, left)
                right = jnp.where(here, pltpu.roll(b, (k + 16) % 128, 1) if k != 112 else b, right)
        ML[pl.ds(i * 8, 8), :] = left
        MR[pl.ds(i * 8, 8), :] = right
    sems = (ms, mr)
    halo_m = [
        remote(ML, NR, sems, 0, {"gx": west}),
        remote(MR, NL, sems, 1, {"gx": east}),
        remote(M.at[:, two, first16], M.at[:, two, above], sems, 2, {"gy": south}),
        remote(M.at[:, two, last16], M.at[:, two, below], sems, 3, {"gy": north}),
        remote(ML.at[pl.ds(0, 16)], KR.at[1], sems, 4, {"gy": south, "gx": west}),
        remote(MR.at[pl.ds(0, 16)], KL.at[1], sems, 5, {"gy": south, "gx": east}),
        remote(ML.at[pl.ds(48, 16)], KR.at[0], sems, 6, {"gy": north, "gx": west}),
        remote(MR.at[pl.ds(48, 16)], KL.at[0], sems, 7, {"gy": north, "gx": east}),
    ]
    for c in halo_m:
        c.start()

    def coefficients(t, row0, rows):
        at = pl.ds(row0, rows)
        inertia = M[0, t, at, :] + 0.5
        w = S[WET, t, at, :] / (inertia + 0.24)
        cA[t, at, :] = w * inertia
        cB[t, at, :] = 0.075 * w
        cG[0, t, at, :] = 0.3 * w * S[FU, t, at, :]
        cG[1, t, at, :] = 0.3 * w * S[FV, t, at, :]
        cK[t, at, :] = M[1, t, at, :] * (1.0 / 6.0)

    @pl.loop(0, 4)
    def _(i):
        for t in range(2):
            coefficients(t, pl.multiple_of(OWN + i * 64, 8), 64)

    for c in halo_m:
        c.wait_recv()
    for c in s1s:
        c.start()
    for f in range(2):
        for chunk in range(4):
            k = 32 * chunk + 16 * f
            for i in range(8):
                at = pl.ds(OWN + chunk * 64 + i * 8, 8)
                raw = pl.ds(i * 8, 8)
                M[f, 2, at, :] = beside(NR[raw, :], NL[raw, :], (128 - k) % 128, (112 - k) % 128)
        for i in range(2):
            raw = pl.ds(i * 8, 8)
            k = 96 + 16 * f
            M[f, 2, pl.ds(8 + i * 8, 8), :] = beside(KR[0, raw, :], KL[0, raw, :], 128 - k, (112 - k) % 128)
            k = 16 * f
            M[f, 2, pl.ds(280 + i * 8, 8), :] = beside(KR[1, raw, :], KL[1, raw, :], (128 - k) % 128, 112 - k)
    clear_outside(M, 2)

    for t in range(2):
        coefficients(t, 8, 16)
        coefficients(t, 280, 16)

    @pl.loop(0, 4)
    def _(i):
        coefficients(2, pl.multiple_of(8 + i * 72, 8), 72)

    for c in halo:
        c.wait_send()
    R = 288
    wide = lax.broadcasted_iota(jnp.int32, (R, 128), 1)
    is_last, is_first = wide == 127, wide == 0

    def across(f, at):
        v = [S[f, t, at, :] for t in range(3)]
        up = [pltpu.roll(a, 127, 1) for a in v]
        down = [pltpu.roll(a, 1, 1) for a in v]
        return [
            jnp.where(is_last, up[(t + 1) % 3], up[t]) - jnp.where(is_first, down[(t + 2) % 3], down[t])
            for t in range(3)
        ]

    def along(f, t, row0):
        return S[f, t, pl.ds(row0 + 1, R), :] - S[f, t, pl.ds(row0 - 1, R), :]

    @pl.loop(0, NSUB)
    def _(n):
        @pl.loop(0, 288 // R)
        def _(i):
            row0 = pl.multiple_of(i * R + 8, 8)
            at = pl.ds(row0, R)
            ux, vx = across(U, at), across(V, at)
            for t in range(3):
                a, b = ux[t], along(V, t, row0)
                sh = along(U, t, row0) + vx[t]
                d, e = a + b, a - b
                k = cK[t, at, :]
                d4 = 4.0 * d
                q = d * d4 + e * e + (sh * sh + 0.64)
                f = k * lax.rsqrt(q)
                k2 = k + k
                S[X, t, at, :] = S[X, t, at, :] * (1.0 / 1.5) + (f * (d4 + e) - k2)
                S[Y, t, at, :] = S[Y, t, at, :] * (1.0 / 1.5) + (f * (d4 - e) - k2)
                S[H, t, at, :] = S[H, t, at, :] * (1.0 / 1.5) + (f + f) * sh

        @pl.loop(0, 288 // R)
        def _(i):
            row0 = pl.multiple_of(i * R + 8, 8)
            at = pl.ds(row0, R)
            xx, hx = across(X, at), across(H, at)
            for t in range(3):
                a, b = cA[t, at, :], cB[t, at, :]
                fe = xx[t] + along(H, t, row0)
                fn = hx[t] + along(Y, t, row0)
                S[U, t, at, :] = a * S[U, t, at, :] + (b * fe + cG[0, t, at, :])
                S[V, t, at, :] = a * S[V, t, at, :] + (b * fn + cG[1, t, at, :])

    @pl.loop(0, 4)
    def _(i):
        at = pl.ds(pl.multiple_of(OWN + i * 64, 8), 64)
        raw = pl.ds(pl.multiple_of(i * 64, 8), 64)
        for t in range(2):
            a, b = S[X, t, at, :], S[Y, t, at, :]
            outb[0, t, raw, :] = 0.5 * (a + b)
            outb[1, t, raw, :] = 0.5 * (a - b)
            outb[2, t, raw, :] = 0.5 * S[H, t, at, :]

    for t in range(2):
        lanes = pl.ds(t * 128, 128)
        store(S.at[pl.ds(U, 2), t, pl.ds(OWN, 256)], velo_hbm.at[:, :, lanes])
        store(outb.at[:, t], stro_hbm.at[:, :, lanes])

    for c in s1s:
        c.wait_recv()
    for k in range(32):
        got[2, k] = rs1[pl.ds(k * 32, 32), :]
    for b in range(NBLK):
        s1, cover = got[2, slot_of[b]], got[1, slot_of[b]]
        temp_b, cool_b = sea[b], air[b]
        for half in range(2):
            part = slice(half * 16, half * 16 + 16)
            lanes = slice(half * 128, half * 128 + 128)
            basal = 0.5 * (temp_b[:, lanes] + 1.8)
            flux[1, half, pl.ds(b * 16, 16), :] = 0.4 * (basal * cover[part] - 0.5 * cool_b[:, lanes] * s1[part])
    for t in range(2):
        store(flux.at[:, t], flux_hbm.at[:, :, pl.ds(t * 128, 128)])
    for c in sends + covs + masses + s1s + halo_m:
        c.wait_send()
    for c in stores:
        c.wait()


def hand_over(nt, flux, velo, stro, nt_out, flux_out, velo_out, stro_out, nt_v, flux_v, velo_v, stro_v, sem):
    parts = [(nt.at[c], nt_v.at[c], nt_out.at[c]) for c in range(NCAT)]
    parts += [(stro.at[c], stro_v.at[c], stro_out.at[c]) for c in range(3)]
    parts += [(velo.at[c], velo_v.at[c], velo_out.at[c]) for c in range(2)]
    parts += [(flux.at[c], flux_v.at[c], flux_out.at[c]) for c in range(2)]
    reads = [pltpu.make_async_copy(a, v, sem.at[0, i]) for i, (a, v, _) in enumerate(parts)]
    writes = [pltpu.make_async_copy(v, b, sem.at[1, i]) for i, (_, v, b) in enumerate(parts)]
    for c in reads:
        c.start()
    for c, d in zip(reads, writes):
        c.wait()
        d.start()
    for d in writes:
        d.wait()


def local(sea, air, cur, wind, land, vel, stress, owner, thick, area, pres):
    any_ = pl.BlockSpec(memory_space=pl.ANY)
    vm = lambda *shape, dtype=F32: pltpu.VMEM(shape, dtype)
    dma = lambda n: pltpu.SemaphoreType.DMA((n,))
    results = (
        jax.ShapeDtypeStruct((NCAT, 32, 4096), F32),
        jax.ShapeDtypeStruct((2, 256, 256), F32),
        jax.ShapeDtypeStruct((2, 256, 256), F32),
        jax.ShapeDtypeStruct((3, 256, 256), F32),
    )
    made = pl.pallas_call(
        kernel,
        out_shape=results,
        in_specs=[pl.BlockSpec(memory_space=pltpu.SMEM)] + [any_] * 10,
        out_specs=(any_,) * 4,
        scratch_shapes=[
            vm(16, 16, 256), vm(16, 16, 256),
            vm(NCAT, 32, 4096), vm(NCAT, 32, 4096), vm(NCAT, 32, 4096, dtype=jnp.int32),
            vm(NCAT, 32, 4096), vm(NCAT, 32, 4096),
            vm(2, 2, 256, 128), vm(2, 2, 256, 128), vm(2, 256, 128, dtype=jnp.int32),
            vm(15 * 128, 128), vm(16 * 128, 128),
            vm(1024, 128), vm(1024, 128), vm(1024, 128),
            vm(1024, 128), vm(1024, 128), vm(1024, 128), vm(3, 32, 32, 128),
            vm(8, 3, ROWS, 128), vm(2, 3, ROWS, 128),
            vm(256, 128), vm(256, 128), vm(288, 128), vm(288, 128),
            vm(64, 128), vm(64, 128), vm(64, 128), vm(64, 128), vm(2, 16, 128), vm(2, 16, 128),
            vm(2, 2, 256, 128),
            vm(3, ROWS, 128), vm(3, ROWS, 128), vm(2, 3, ROWS, 128), vm(3, ROWS, 128),
            vm(3, 2, 256, 128),
            dma(15), dma(10),
            dma(15), dma(15), dma(15), dma(15), dma(15), dma(15), dma(15), dma(15),
            dma(8), dma(8), dma(8), dma(8),
        ],
        compiler_params=pltpu.CompilerParams(
            collective_id=0, has_side_effects=True, vmem_limit_bytes=60 * 1024 * 1024
        ),
    )(
        owner, sea.reshape(16, 16, 256), air.reshape(16, 16, 256), cur, wind, land, vel, stress,
        thick.reshape(NCAT, 32, 4096), area.reshape(NCAT, 32, 4096), pres.reshape(NCAT, 32, 4096),
    )
    nt, flux, velo, stro = pl.pallas_call(
        hand_over,
        out_shape=results,
        in_specs=[any_] * 4,
        out_specs=(any_,) * 4,
        scratch_shapes=[vm(*o.shape) for o in results] + [pltpu.SemaphoreType.DMA((2, 12))],
        compiler_params=pltpu.CompilerParams(vmem_limit_bytes=60 * 1024 * 1024),
    )(*made)
    return nt.reshape(NCAT, 1, 32, 4096), flux, velo, stro


def solution(mesh):
    grid, pair, ice = P("gy", "gx"), P(None, "gy", "gx"), P(None, "gy", "gx", None)
    return jax.shard_map(
        local,
        mesh=mesh,
        in_specs=(grid, grid, pair, pair, grid, pair, pair, grid, ice, ice, ice),
        out_specs=(ice, pair, pair, pair),
        check_vma=False,
    )
```

```python
import functools

import jax
import jax.numpy as jnp
from jax import lax
from jax.experimental import pallas as pl
from jax.experimental.pallas import tpu as pltpu
from jax.sharding import PartitionSpec as P

F32 = jnp.float32
MESH = pl.DeviceIdType.MESH
NSUB = 8
NCAT = 5
NBLK = 16
STEPS = (
    (1, 2), (0, 2), (2, 1), (2, 0), (3, 2), (0, 1), (2, 3), (1, 0),
    (2, 2), (0, 3), (1, 1), (3, 0), (3, 3), (1, 3), (3, 1),
)
ROWS = 304
OWN = 24
NO_BLOCK = 1.0e6
U, V, X, Y, H, FU, FV, WET = range(8)


def kernel(
    owner_ref, sea_hbm, air_hbm, cur_hbm, wind_hbm, land_hbm, vel_hbm, str_hbm, thick_hbm, area_hbm, pres_hbm,
    nt_hbm, flux_hbm, velo_hbm, stro_hbm,
    sea, air, thick, area, pres, rc, nt, wind, cur, land,
    snd, rcv, scov, smass, ss1, rcov, rmass, rs1, got,
    S, M, PL, PR, QL, QR, ML, MR, NL, NR, KL, KR, flux,
    cA, cB, cG, cK, outb,
    lsem, osem, snd_s, snd_r, cov_s, cov_r, mass_s, mass_r, s1_s, s1_r, hs, hr, ms, mr,
):
    r = lax.axis_index("gy")
    s = lax.axis_index("gx")
    z, x = s // 4, s % 4

    odd = r % 2

    def dev(dz, dx):
        dz, dx = dz + odd * (dx - dz), dx + odd * (dz - dx)
        return ((z + dz) % 4) * 4 + (x + dx) % 4

    loads = {}

    def load(name, src, dst):
        c = pltpu.make_async_copy(src, dst, lsem.at[len(loads)])
        c.start()
        loads[name] = c

    load("sea", sea_hbm, sea)
    load("air", air_hbm, air)
    barrier = pltpu.get_barrier_semaphore()
    north, south = (r + 1) % 8, (r + 7) % 8
    east, west = (s + 1) % 16, (s + 15) % 16
    for dz, dx in STEPS:
        pl.semaphore_signal(barrier, inc=1, device_id={"gx": dev(dz, dx)}, device_id_type=MESH)
    for ry in (north, south):
        for sx in (west, s, east):
            pl.semaphore_signal(barrier, inc=1, device_id={"gy": ry, "gx": sx}, device_id_type=MESH)

    load("thick", thick_hbm, thick)
    load("area", area_hbm, area)
    load("pres", pres_hbm, pres)
    for t in range(2):
        lanes = pl.ds(t * 128, 128)
        load(("vel", t), vel_hbm.at[:, :, lanes], S.at[pl.ds(U, 2), t, pl.ds(OWN, 256)])
        load(("str", t), str_hbm.at[:, :, lanes], S.at[pl.ds(X, 3), t, pl.ds(OWN, 256)])
        load(("wind", t), wind_hbm.at[:, :, lanes], wind.at[:, t])
        load(("cur", t), cur_hbm.at[:, :, lanes], cur.at[:, t])
        load(("land", t), land_hbm.at[:, lanes], land.at[t])

    owners = [owner_ref[0, b] for b in range(NBLK)]
    spare = jnp.zeros((8, 128), F32)
    for f in range(5):
        for t in range(3):
            S[f, t, pl.ds(0, 8), :] = spare
            S[f, t, pl.ds(ROWS - 8, 8), :] = spare

    loads["sea"].wait()
    loads["air"].wait()

    def stage(buf, row0, target):
        hits = [(owners[b] == target).astype(jnp.int32) for b in range(NBLK)]
        count = hits[0]
        first = last = hits[0] * 0
        for b in range(1, NBLK):
            first = first + hits[b] * (1 - jnp.minimum(count, 1)) * b
            last = last + hits[b] * (b - last)
            count = count + hits[b]
        for k, b in ((0, first), (1, last)):
            filled = (count > k).astype(jnp.int32).astype(F32)
            temp_b = sea[b] * filled + NO_BLOCK * (1.0 - filled)
            cool_b = air[b]
            for half in range(2):
                at = row0 + k * 64 + half * 16
                buf[pl.ds(at, 16), :] = temp_b[:, half * 128 : half * 128 + 128]
                buf[pl.ds(at + 32, 16), :] = cool_b[:, half * 128 : half * 128 + 128]

    for i, (dz, dx) in enumerate(STEPS):
        stage(snd, i * 128, dev(dz, dx))
    pl.semaphore_wait(barrier, 21)
    sends = []
    for i, (dz, dx) in enumerate(STEPS):
        target = dev(dz, dx)
        c = pltpu.make_async_remote_copy(
            src_ref=snd.at[pl.ds(i * 128, 128)], dst_ref=rcv.at[pl.ds(pl.multiple_of(s * 128, 128), 128)],
            send_sem=snd_s.at[i], recv_sem=snd_r.at[i], device_id={"gx": target}, device_id_type=MESH,
        )
        c.start()
        sends.append(c)
    stage(rcv, pl.multiple_of(s * 128, 128), s)

    for n in ("thick", "area", "pres"):
        loads[n].wait()

    def prepare(g, row, half):
        lanes = pl.ds(pl.multiple_of(row * 256 + half * 128, 128), 128)
        slots = pl.ds(pl.multiple_of(g * 8, 8), 8)
        cover = jnp.zeros((8, 128), F32)
        s1 = jnp.zeros((8, 128), F32)
        for c in range(NCAT):
            p = pres[c, slots, lanes].astype(F32)
            tl = thick[c, slots, lanes] * p
            al = area[c, slots, lanes] * p
            inv = 1.0 / (tl + 0.5)
            thick[c, slots, lanes] = tl
            area[c, slots, lanes] = al
            rc[c, slots, lanes] = inv
            cover = cover + al
            s1 = s1 + al * inv
        at = g * 256 + half * 16 + row
        scov[pl.ds(at, 8, stride=32), :] = cover
        ss1[pl.ds(at, 8, stride=32), :] = s1

    @pl.loop(0, 64)
    def _(i):
        for half in range(2):
            prepare(i // 16, i % 16, half)

    def back(buf, dst, ssem, rsem, i):
        dz, dx = STEPS[i]
        target = dev(-dz, -dx)
        return pltpu.make_async_remote_copy(
            src_ref=buf.at[pl.ds(pl.multiple_of(target * 64, 64), 64)],
            dst_ref=dst.at[pl.ds(pl.multiple_of(s * 64, 64), 64)],
            send_sem=ssem.at[i], recv_sem=rsem.at[i], device_id={"gx": target}, device_id_type=MESH,
        )

    covs = [back(scov, rcov, cov_s, cov_r, i) for i in range(15)]
    for c in covs:
        c.start()
    mine = pl.ds(pl.multiple_of(s * 64, 64), 64)
    rcov[mine, :] = scov[mine, :]
    rs1[mine, :] = ss1[mine, :]

    for t in range(2):
        for n in ("vel", "str", "wind", "cur", "land"):
            loads[(n, t)].wait()

    lane = lax.broadcasted_iota(jnp.int32, (8, 128), 1)
    own_rows = lambda i: pl.ds(pl.multiple_of(OWN + i * 8, 8), 8)

    @pl.loop(0, 32)
    def _(i):
        at = own_rows(i)
        raw = pl.ds(pl.multiple_of(i * 8, 8), 8)
        fields = []
        for t in range(2):
            total, diff = S[X, t, at, :], S[Y, t, at, :]
            S[X, t, at, :] = total + diff
            S[Y, t, at, :] = total - diff
            S[H, t, at, :] = 2.0 * S[H, t, at, :]
            S[FU, t, at, :] = wind[0, t, raw, :] + 0.8 * cur[0, t, raw, :]
            S[FV, t, at, :] = wind[1, t, raw, :] + 0.8 * cur[1, t, raw, :]
            S[WET, t, at, :] = 1.0 - land[t, raw, :].astype(F32)
        left = S[0, 0, at, :]
        right = pltpu.roll(S[0, 1, at, :], 16, 1)
        for f in range(1, 8):
            here = (lane >= 16 * f) & (lane < 16 * f + 16)
            left = jnp.where(here, pltpu.roll(S[f, 0, at, :], 16 * f, 1), left)
            last = S[f, 1, at, :]
            right = jnp.where(here, pltpu.roll(last, 16 * f + 16, 1) if f < 7 else last, right)
        PL[raw, :] = left
        PR[raw, :] = right

    first16, last16 = pl.ds(OWN, 16), pl.ds(OWN + 240, 16)
    above, below = pl.ds(280, 16), pl.ds(8, 16)

    def remote(src, dst, sems, n, to):
        return pltpu.make_async_remote_copy(
            src_ref=src, dst_ref=dst, send_sem=sems[0].at[n], recv_sem=sems[1].at[n],
            device_id=to, device_id_type=MESH,
        )

    two = pl.ds(0, 2)
    sems = (hs, hr)
    halo = [
        remote(PL, QR.at[pl.ds(16, 256)], sems, 0, {"gx": west}),
        remote(PR, QL.at[pl.ds(16, 256)], sems, 1, {"gx": east}),
        remote(S.at[:, two, first16], S.at[:, two, above], sems, 2, {"gy": south}),
        remote(S.at[:, two, last16], S.at[:, two, below], sems, 3, {"gy": north}),
        remote(PL.at[pl.ds(0, 16)], QR.at[pl.ds(272, 16)], sems, 4, {"gy": south, "gx": west}),
        remote(PR.at[pl.ds(0, 16)], QL.at[pl.ds(272, 16)], sems, 5, {"gy": south, "gx": east}),
        remote(PL.at[pl.ds(240, 16)], QR.at[pl.ds(0, 16)], sems, 6, {"gy": north, "gx": west}),
        remote(PR.at[pl.ds(240, 16)], QL.at[pl.ds(0, 16)], sems, 7, {"gy": north, "gx": east}),
    ]
    for c in halo:
        c.start()

    for c in sends:
        c.wait_recv()

    def grow(g, row, half):
        lanes = pl.ds(pl.multiple_of(row * 256 + half * 128, 128), 128)
        slots = pl.ds(pl.multiple_of(g * 8, 8), 8)
        at = g * 512 + half * 16 + row
        heat_in = 0.2 * (rcv[pl.ds(at, 8, stride=64), :] + 1.8)
        cool_in = 0.2 * rcv[pl.ds(at + 32, 8, stride=64), :]
        mass = jnp.zeros((8, 128), F32)
        for c in range(NCAT):
            change = cool_in * rc[c, slots, lanes] - heat_in
            grown = jnp.maximum(thick[c, slots, lanes] + change, 0.0)
            mass = mass + area[c, slots, lanes] * grown
            nt[c, slots, lanes] = pres[c, slots, lanes].astype(F32) * grown
        smass[pl.ds(g * 256 + half * 16 + row, 8, stride=32), :] = mass

    @pl.loop(0, 32)
    def _(i):
        for k in range(2):
            for half in range(2):
                grow(i // 8, (i % 8) * 2 + k, half)

    masses = [back(smass, rmass, mass_s, mass_r, i) for i in range(15)]
    for c in masses:
        c.start()
    stores = []

    def store(src, dst):
        c = pltpu.make_async_copy(src, dst, osem.at[len(stores)])
        c.start()
        stores.append(c)

    store(nt, nt_hbm)
    rmass[mine, :] = smass[mine, :]
    s1s = [back(ss1, rs1, s1_s, s1_r, i) for i in range(15)]

    at_west, at_east = s == 0, s == 15
    at_south, at_north = r == 0, r == 7
    for c in halo:
        c.wait_recv()

    def beside(right, left, shift_right, shift_left):
        a = jnp.where(at_east, 0.0, pltpu.roll(right, shift_right, 1) if shift_right else right)
        b = jnp.where(at_west, 0.0, pltpu.roll(left, shift_left, 1) if shift_left else left)
        return jnp.where(lane < 16, a, jnp.where(lane >= 112, b, 0.0))

    @pl.loop(0, 36)
    def _(i):
        raw = pl.ds(pl.multiple_of(i * 8, 8), 8)
        at = pl.ds(pl.multiple_of(i * 8 + 8, 8), 8)
        right, left = QR[raw, :], QL[raw, :]
        for f in range(8):
            S[f, 2, at, :] = beside(right, left, (128 - 16 * f) % 128, (112 - 16 * f) % 128)

    def clear_outside(ref, n):
        for at, gone in ((below, at_south), (above, at_north)):
            for f in range(n):
                for t in range(3):
                    ref[f, t, at, :] = jnp.where(gone, 0.0, ref[f, t, at, :])

    clear_outside(S, 8)

    slot_of = []
    for b in range(NBLK):
        slot = owners[b] * 2
        for e in range(b):
            slot = slot + (owners[e] == owners[b]).astype(jnp.int32)
        slot_of.append(slot)
    for c in covs:
        c.wait_recv()
    for k in range(32):
        got[1, k] = rcov[pl.ds(k * 32, 32), :]
    for b in range(NBLK):
        cover = got[1, slot_of[b]]
        damping = jnp.exp(-2.0 * (1.0 - cover))
        temp_b, cool_b = sea[b], air[b]
        for half in range(2):
            part = slice(half * 16, half * 16 + 16)
            lanes = slice(half * 128, half * 128 + 128)
            cv = cover[part]
            M[1, half, pl.ds(OWN + b * 16, 16), :] = damping[part]
            flux[0, half, pl.ds(b * 16, 16), :] = cv * (0.5 * (temp_b[:, lanes] + 1.8)) - (1.0 - cv) * cool_b[:, lanes]
    for c in masses:
        c.wait_recv()
    for k in range(32):
        got[0, k] = rmass[pl.ds(k * 32, 32), :]
    for b in range(NBLK):
        mass = got[0, slot_of[b]]
        for half in range(2):
            rows = pl.ds(OWN + b * 16, 16)
            part = mass[half * 16 : half * 16 + 16]
            M[0, half, rows, :] = part
            M[1, half, rows, :] = M[1, half, rows, :] * part

    for i in range(8):
        left = jnp.zeros((8, 128), F32)
        right = left
        for chunk in range(4):
            for f in range(2):
                at = pl.ds(OWN + chunk * 64 + i * 8, 8)
                k = 32 * chunk + 16 * f
                here = (lane >= k) & (lane < k + 16)
                a, b = M[f, 0, at, :], M[f, 1, at, :]
                left = jnp.where(here, pltpu.roll(a, k, 1) if k else a, left)
                right = jnp.where(here, pltpu.roll(b, (k + 16) % 128, 1) if k != 112 else b, right)
        ML[pl.ds(i * 8, 8), :] = left
        MR[pl.ds(i * 8, 8), :] = right
    sems = (ms, mr)
    halo_m = [
        remote(ML, NR, sems, 0, {"gx": west}),
        remote(MR, NL, sems, 1, {"gx": east}),
        remote(M.at[:, two, first16], M.at[:, two, above], sems, 2, {"gy": south}),
        remote(M.at[:, two, last16], M.at[:, two, below], sems, 3, {"gy": north}),
        remote(ML.at[pl.ds(0, 16)], KR.at[1], sems, 4, {"gy": south, "gx": west}),
        remote(MR.at[pl.ds(0, 16)], KL.at[1], sems, 5, {"gy": south, "gx": east}),
        remote(ML.at[pl.ds(48, 16)], KR.at[0], sems, 6, {"gy": north, "gx": west}),
        remote(MR.at[pl.ds(48, 16)], KL.at[0], sems, 7, {"gy": north, "gx": east}),
    ]
    for c in halo_m:
        c.start()

    def coefficients(t, row0, rows):
        at = pl.ds(row0, rows)
        inertia = M[0, t, at, :] + 0.5
        w = S[WET, t, at, :] / (inertia + 0.24)
        cA[t, at, :] = w * inertia
        cB[t, at, :] = 0.075 * w
        cG[0, t, at, :] = 0.3 * w * S[FU, t, at, :]
        cG[1, t, at, :] = 0.3 * w * S[FV, t, at, :]
        cK[t, at, :] = M[1, t, at, :] * (1.0 / 6.0)

    @pl.loop(0, 4)
    def _(i):
        for t in range(2):
            coefficients(t, pl.multiple_of(OWN + i * 64, 8), 64)

    def across(f, row0, rows, tiles):
        wide = lax.broadcasted_iota(jnp.int32, (rows, 128), 1)
        v = [S[f, t, pl.ds(row0, rows), :] for t in range(3)]
        up = [pltpu.roll(a, 127, 1) for a in v]
        down = [pltpu.roll(a, 1, 1) for a in v]
        return {
            t: jnp.where(wide == 127, up[(t + 1) % 3], up[t]) - jnp.where(wide == 0, down[(t + 2) % 3], down[t])
            for t in tiles
        }

    def along(f, t, row0, rows):
        return S[f, t, pl.ds(row0 + 1, rows), :] - S[f, t, pl.ds(row0 - 1, rows), :]

    def relax(row0, rows, tiles=(0, 1, 2)):
        at = pl.ds(row0, rows)
        ux, vx = across(U, row0, rows, tiles), across(V, row0, rows, tiles)
        for t in tiles:
            a, b = ux[t], along(V, t, row0, rows)
            sh = along(U, t, row0, rows) + vx[t]
            d, e = a + b, a - b
            k = cK[t, at, :]
            d4 = 4.0 * d
            q = d * d4 + e * e + (sh * sh + 0.64)
            f = k * lax.rsqrt(q)
            k2 = k + k
            S[X, t, at, :] = S[X, t, at, :] * (1.0 / 1.5) + (f * (d4 + e) - k2)
            S[Y, t, at, :] = S[Y, t, at, :] * (1.0 / 1.5) + (f * (d4 - e) - k2)
            S[H, t, at, :] = S[H, t, at, :] * (1.0 / 1.5) + (f + f) * sh

    def move(row0, rows, tiles=(0, 1, 2)):
        at = pl.ds(row0, rows)
        xx, hx = across(X, row0, rows, tiles), across(H, row0, rows, tiles)
        for t in tiles:
            a, b = cA[t, at, :], cB[t, at, :]
            fe = xx[t] + along(H, t, row0, rows)
            fn = hx[t] + along(Y, t, row0, rows)
            S[U, t, at, :] = a * S[U, t, at, :] + (b * fe + cG[0, t, at, :])
            S[V, t, at, :] = a * S[V, t, at, :] + (b * fn + cG[1, t, at, :])

    for c in s1s[:8]:
        c.start()
    for c in halo:
        c.wait_send()

    @pl.loop(0, 4)
    def _(i):
        relax(pl.multiple_of(OWN + i * 64, 8), 64, (0, 1))

    for c in halo_m:
        c.wait_recv()
    for c in s1s[8:]:
        c.start()
    for f in range(2):
        for chunk in range(4):
            k = 32 * chunk + 16 * f
            for i in range(8):
                at = pl.ds(OWN + chunk * 64 + i * 8, 8)
                raw = pl.ds(i * 8, 8)
                M[f, 2, at, :] = beside(NR[raw, :], NL[raw, :], (128 - k) % 128, (112 - k) % 128)
        for i in range(2):
            raw = pl.ds(i * 8, 8)
            k = 96 + 16 * f
            M[f, 2, pl.ds(8 + i * 8, 8), :] = beside(KR[0, raw, :], KL[0, raw, :], 128 - k, (112 - k) % 128)
            k = 16 * f
            M[f, 2, pl.ds(280 + i * 8, 8), :] = beside(KR[1, raw, :], KL[1, raw, :], (128 - k) % 128, 112 - k)
    clear_outside(M, 2)

    for t in range(2):
        coefficients(t, 8, 16)
        coefficients(t, 280, 16)

    @pl.loop(0, 4)
    def _(i):
        coefficients(2, pl.multiple_of(8 + i * 72, 8), 72)

    for t in range(2):
        relax(8, 16, (t,))
        relax(280, 16, (t,))

    @pl.loop(0, 3)
    def _(i):
        relax(pl.multiple_of(8 + i * 96, 8), 96, (2,))

    @pl.loop(1, NSUB)
    def _(n):
        move(8, 288)
        relax(8, 288)

    @pl.loop(0, 4)
    def _(i):
        move(pl.multiple_of(OWN + i * 64, 8), 64, (0, 1))

    @pl.loop(0, 4)
    def _(i):
        at = pl.ds(pl.multiple_of(OWN + i * 64, 8), 64)
        raw = pl.ds(pl.multiple_of(i * 64, 8), 64)
        for t in range(2):
            a, b = S[X, t, at, :], S[Y, t, at, :]
            outb[0, t, raw, :] = 0.5 * (a + b)
            outb[1, t, raw, :] = 0.5 * (a - b)
            outb[2, t, raw, :] = 0.5 * S[H, t, at, :]

    for t in range(2):
        lanes = pl.ds(t * 128, 128)
        store(S.at[pl.ds(U, 2), t, pl.ds(OWN, 256)], velo_hbm.at[:, :, lanes])
        store(outb.at[:, t], stro_hbm.at[:, :, lanes])

    for c in s1s:
        c.wait_recv()
    for k in range(32):
        got[2, k] = rs1[pl.ds(k * 32, 32), :]
    for b in range(NBLK):
        s1, cover = got[2, slot_of[b]], got[1, slot_of[b]]
        temp_b, cool_b = sea[b], air[b]
        for half in range(2):
            part = slice(half * 16, half * 16 + 16)
            lanes = slice(half * 128, half * 128 + 128)
            basal = 0.5 * (temp_b[:, lanes] + 1.8)
            flux[1, half, pl.ds(b * 16, 16), :] = 0.4 * (basal * cover[part] - 0.5 * cool_b[:, lanes] * s1[part])
    for t in range(2):
        store(flux.at[:, t], flux_hbm.at[:, :, pl.ds(t * 128, 128)])
    for c in sends + covs + masses + s1s + halo_m:
        c.wait_send()
    for c in stores:
        c.wait()


def hand_over(nt, flux, velo, stro, nt_out, flux_out, velo_out, stro_out, nt_v, flux_v, velo_v, stro_v, sem):
    parts = [(nt.at[c], nt_v.at[c], nt_out.at[c]) for c in range(NCAT)]
    parts += [(stro.at[c], stro_v.at[c], stro_out.at[c]) for c in range(3)]
    parts += [(velo.at[c], velo_v.at[c], velo_out.at[c]) for c in range(2)]
    parts += [(flux.at[c], flux_v.at[c], flux_out.at[c]) for c in range(2)]
    reads = [pltpu.make_async_copy(a, v, sem.at[0, i]) for i, (a, v, _) in enumerate(parts)]
    writes = [pltpu.make_async_copy(v, b, sem.at[1, i]) for i, (_, v, b) in enumerate(parts)]
    for c in reads:
        c.start()
    for c, d in zip(reads, writes):
        c.wait()
        d.start()
    for d in writes:
        d.wait()


def local(sea, air, cur, wind, land, vel, stress, owner, thick, area, pres):
    any_ = pl.BlockSpec(memory_space=pl.ANY)
    vm = lambda *shape, dtype=F32: pltpu.VMEM(shape, dtype)
    dma = lambda n: pltpu.SemaphoreType.DMA((n,))
    results = (
        jax.ShapeDtypeStruct((NCAT, 32, 4096), F32),
        jax.ShapeDtypeStruct((2, 256, 256), F32),
        jax.ShapeDtypeStruct((2, 256, 256), F32),
        jax.ShapeDtypeStruct((3, 256, 256), F32),
    )
    made = pl.pallas_call(
        kernel,
        out_shape=results,
        in_specs=[pl.BlockSpec(memory_space=pltpu.SMEM)] + [any_] * 10,
        out_specs=(any_,) * 4,
        scratch_shapes=[
            vm(16, 16, 256), vm(16, 16, 256),
            vm(NCAT, 32, 4096), vm(NCAT, 32, 4096), vm(NCAT, 32, 4096, dtype=jnp.int32),
            vm(NCAT, 32, 4096), vm(NCAT, 32, 4096),
            vm(2, 2, 256, 128), vm(2, 2, 256, 128), vm(2, 256, 128, dtype=jnp.int32),
            vm(15 * 128, 128), vm(16 * 128, 128),
            vm(1024, 128), vm(1024, 128), vm(1024, 128),
            vm(1024, 128), vm(1024, 128), vm(1024, 128), vm(3, 32, 32, 128),
            vm(8, 3, ROWS, 128), vm(2, 3, ROWS, 128),
            vm(256, 128), vm(256, 128), vm(288, 128), vm(288, 128),
            vm(64, 128), vm(64, 128), vm(64, 128), vm(64, 128), vm(2, 16, 128), vm(2, 16, 128),
            vm(2, 2, 256, 128),
            vm(3, ROWS, 128), vm(3, ROWS, 128), vm(2, 3, ROWS, 128), vm(3, ROWS, 128),
            vm(3, 2, 256, 128),
            dma(15), dma(10),
            dma(15), dma(15), dma(15), dma(15), dma(15), dma(15), dma(15), dma(15),
            dma(8), dma(8), dma(8), dma(8),
        ],
        compiler_params=pltpu.CompilerParams(
            collective_id=0, has_side_effects=True, vmem_limit_bytes=60 * 1024 * 1024
        ),
    )(
        owner, sea.reshape(16, 16, 256), air.reshape(16, 16, 256), cur, wind, land, vel, stress,
        thick.reshape(NCAT, 32, 4096), area.reshape(NCAT, 32, 4096), pres.reshape(NCAT, 32, 4096),
    )
    nt, flux, velo, stro = pl.pallas_call(
        hand_over,
        out_shape=results,
        in_specs=[any_] * 4,
        out_specs=(any_,) * 4,
        scratch_shapes=[vm(*o.shape) for o in results] + [pltpu.SemaphoreType.DMA((2, 12))],
        compiler_params=pltpu.CompilerParams(vmem_limit_bytes=60 * 1024 * 1024),
    )(*made)
    return nt.reshape(NCAT, 1, 32, 4096), flux, velo, stro


def solution(mesh):
    grid, pair, ice = P("gy", "gx"), P(None, "gy", "gx"), P(None, "gy", "gx", None)
    return jax.shard_map(
        local,
        mesh=mesh,
        in_specs=(grid, grid, pair, pair, grid, pair, pair, grid, ice, ice, ice),
        out_specs=(ice, pair, pair, pair),
        check_vma=False,
    )
```

```python
import functools

import jax
import jax.numpy as jnp
from jax import lax
from jax.experimental import pallas as pl
from jax.experimental.pallas import tpu as pltpu
from jax.sharding import PartitionSpec as P

F32 = jnp.float32
MESH = pl.DeviceIdType.MESH
NSUB = 8
NCAT = 5
NBLK = 16
STEPS = (
    (1, 2), (0, 2), (2, 1), (2, 0), (3, 2), (0, 1), (2, 3), (1, 0),
    (2, 2), (0, 3), (1, 1), (3, 0), (3, 3), (1, 3), (3, 1),
)
ROWS = 304
OWN = 24
NO_BLOCK = 1.0e6
U, V, X, Y, H, FU, FV, WET = range(8)


def kernel(
    owner_ref, sea_hbm, air_hbm, cur_hbm, wind_hbm, land_hbm, vel_hbm, str_hbm, thick_hbm, area_hbm, pres_hbm,
    nt_hbm, flux_hbm, velo_hbm, stro_hbm,
    sea, air, thick, area, pres, rc, nt, wind, cur, land,
    snd, rcv, scov, smass, ss1, rcov, rmass, rs1, got,
    S, M, PL, PR, QL, QR, ML, MR, NL, NR, KL, KR, flux,
    cA, cB, cG, cK, outb,
    lsem, osem, snd_s, snd_r, cov_s, cov_r, mass_s, mass_r, s1_s, s1_r, hs, hr, ms, mr,
):
    r = lax.axis_index("gy")
    s = lax.axis_index("gx")
    z, x = s // 4, s % 4

    odd = r % 2

    def dev(dz, dx, exchange=odd):
        dz, dx = dz + exchange * (dx - dz), dx + exchange * (dz - dx)
        return ((z + dz) % 4) * 4 + (x + dx) % 4

    loads = {}

    def load(name, src, dst):
        c = pltpu.make_async_copy(src, dst, lsem.at[len(loads)])
        c.start()
        loads[name] = c

    load("sea", sea_hbm, sea)
    load("air", air_hbm, air)
    barrier = pltpu.get_barrier_semaphore()
    north, south = (r + 1) % 8, (r + 7) % 8
    east, west = (s + 1) % 16, (s + 15) % 16
    for dz, dx in STEPS:
        pl.semaphore_signal(barrier, inc=1, device_id={"gx": dev(dz, dx)}, device_id_type=MESH)
    for ry in (north, south):
        for sx in (west, s, east):
            pl.semaphore_signal(barrier, inc=1, device_id={"gy": ry, "gx": sx}, device_id_type=MESH)

    load("thick", thick_hbm, thick)
    load("area", area_hbm, area)
    load("pres", pres_hbm, pres)
    for t in range(2):
        lanes = pl.ds(t * 128, 128)
        load(("vel", t), vel_hbm.at[:, :, lanes], S.at[pl.ds(U, 2), t, pl.ds(OWN, 256)])
        load(("str", t), str_hbm.at[:, :, lanes], S.at[pl.ds(X, 3), t, pl.ds(OWN, 256)])
        load(("wind", t), wind_hbm.at[:, :, lanes], wind.at[:, t])
        load(("cur", t), cur_hbm.at[:, :, lanes], cur.at[:, t])
        load(("land", t), land_hbm.at[:, lanes], land.at[t])

    owners = [owner_ref[0, b] for b in range(NBLK)]
    spare = jnp.zeros((8, 128), F32)
    for f in range(5):
        for t in range(3):
            S[f, t, pl.ds(0, 8), :] = spare
            S[f, t, pl.ds(ROWS - 8, 8), :] = spare

    loads["sea"].wait()
    loads["air"].wait()

    def stage(buf, row0, target):
        hits = [(owners[b] == target).astype(jnp.int32) for b in range(NBLK)]
        count = hits[0]
        first = last = hits[0] * 0
        for b in range(1, NBLK):
            first = first + hits[b] * (1 - jnp.minimum(count, 1)) * b
            last = last + hits[b] * (b - last)
            count = count + hits[b]
        for k, b in ((0, first), (1, last)):
            filled = (count > k).astype(jnp.int32).astype(F32)
            temp_b = sea[b] * filled + NO_BLOCK * (1.0 - filled)
            cool_b = air[b]
            for half in range(2):
                at = row0 + k * 64 + half * 16
                buf[pl.ds(at, 16), :] = temp_b[:, half * 128 : half * 128 + 128]
                buf[pl.ds(at + 32, 16), :] = cool_b[:, half * 128 : half * 128 + 128]

    for i, (dz, dx) in enumerate(STEPS):
        stage(snd, i * 128, dev(dz, dx))
    pl.semaphore_wait(barrier, 21)
    sends = []
    for i, (dz, dx) in enumerate(STEPS):
        target = dev(dz, dx)
        c = pltpu.make_async_remote_copy(
            src_ref=snd.at[pl.ds(i * 128, 128)], dst_ref=rcv.at[pl.ds(pl.multiple_of(s * 128, 128), 128)],
            send_sem=snd_s.at[i], recv_sem=snd_r.at[i], device_id={"gx": target}, device_id_type=MESH,
        )
        c.start()
        sends.append(c)
    stage(rcv, pl.multiple_of(s * 128, 128), s)

    for n in ("thick", "area", "pres"):
        loads[n].wait()

    def prepare(g, row, half):
        lanes = pl.ds(pl.multiple_of(row * 256 + half * 128, 128), 128)
        slots = pl.ds(pl.multiple_of(g * 8, 8), 8)
        cover = jnp.zeros((8, 128), F32)
        s1 = jnp.zeros((8, 128), F32)
        for c in range(NCAT):
            p = pres[c, slots, lanes].astype(F32)
            tl = thick[c, slots, lanes] * p
            al = area[c, slots, lanes] * p
            inv = 1.0 / (tl + 0.5)
            thick[c, slots, lanes] = tl
            area[c, slots, lanes] = al
            rc[c, slots, lanes] = inv
            cover = cover + al
            s1 = s1 + al * inv
        at = g * 256 + half * 16 + row
        scov[pl.ds(at, 8, stride=32), :] = cover
        ss1[pl.ds(at, 8, stride=32), :] = s1

    @pl.loop(0, 64)
    def _(i):
        for half in range(2):
            prepare(i // 16, i % 16, half)

    def back(buf, dst, ssem, rsem, i, exchange=odd):
        dz, dx = STEPS[i]
        target = dev(-dz, -dx, exchange)
        return pltpu.make_async_remote_copy(
            src_ref=buf.at[pl.ds(pl.multiple_of(target * 64, 64), 64)],
            dst_ref=dst.at[pl.ds(pl.multiple_of(s * 64, 64), 64)],
            send_sem=ssem.at[i], recv_sem=rsem.at[i], device_id={"gx": target}, device_id_type=MESH,
        )

    covs = [back(scov, rcov, cov_s, cov_r, i) for i in range(15)]
    for c in covs:
        c.start()
    mine = pl.ds(pl.multiple_of(s * 64, 64), 64)
    rcov[mine, :] = scov[mine, :]
    rs1[mine, :] = ss1[mine, :]

    for t in range(2):
        for n in ("vel", "str", "wind", "cur", "land"):
            loads[(n, t)].wait()

    lane = lax.broadcasted_iota(jnp.int32, (8, 128), 1)
    own_rows = lambda i: pl.ds(pl.multiple_of(OWN + i * 8, 8), 8)

    @pl.loop(0, 32)
    def _(i):
        at = own_rows(i)
        raw = pl.ds(pl.multiple_of(i * 8, 8), 8)
        fields = []
        for t in range(2):
            total, diff = S[X, t, at, :], S[Y, t, at, :]
            S[X, t, at, :] = total + diff
            S[Y, t, at, :] = total - diff
            S[H, t, at, :] = 2.0 * S[H, t, at, :]
            S[FU, t, at, :] = wind[0, t, raw, :] + 0.8 * cur[0, t, raw, :]
            S[FV, t, at, :] = wind[1, t, raw, :] + 0.8 * cur[1, t, raw, :]
            S[WET, t, at, :] = 1.0 - land[t, raw, :].astype(F32)
        left = S[0, 0, at, :]
        right = pltpu.roll(S[0, 1, at, :], 16, 1)
        for f in range(1, 8):
            here = (lane >= 16 * f) & (lane < 16 * f + 16)
            left = jnp.where(here, pltpu.roll(S[f, 0, at, :], 16 * f, 1), left)
            last = S[f, 1, at, :]
            right = jnp.where(here, pltpu.roll(last, 16 * f + 16, 1) if f < 7 else last, right)
        PL[raw, :] = left
        PR[raw, :] = right

    first16, last16 = pl.ds(OWN, 16), pl.ds(OWN + 240, 16)
    above, below = pl.ds(280, 16), pl.ds(8, 16)

    def remote(src, dst, sems, n, to):
        return pltpu.make_async_remote_copy(
            src_ref=src, dst_ref=dst, send_sem=sems[0].at[n], recv_sem=sems[1].at[n],
            device_id=to, device_id_type=MESH,
        )

    two = pl.ds(0, 2)
    sems = (hs, hr)
    halo = [
        remote(PL, QR.at[pl.ds(16, 256)], sems, 0, {"gx": west}),
        remote(PR, QL.at[pl.ds(16, 256)], sems, 1, {"gx": east}),
        remote(S.at[:, two, first16], S.at[:, two, above], sems, 2, {"gy": south}),
        remote(S.at[:, two, last16], S.at[:, two, below], sems, 3, {"gy": north}),
        remote(PL.at[pl.ds(0, 16)], QR.at[pl.ds(272, 16)], sems, 4, {"gy": south, "gx": west}),
        remote(PR.at[pl.ds(0, 16)], QL.at[pl.ds(272, 16)], sems, 5, {"gy": south, "gx": east}),
        remote(PL.at[pl.ds(240, 16)], QR.at[pl.ds(0, 16)], sems, 6, {"gy": north, "gx": west}),
        remote(PR.at[pl.ds(240, 16)], QL.at[pl.ds(0, 16)], sems, 7, {"gy": north, "gx": east}),
    ]
    for c in halo:
        c.start()

    for c in sends:
        c.wait_recv()

    def grow(g, row, half):
        lanes = pl.ds(pl.multiple_of(row * 256 + half * 128, 128), 128)
        slots = pl.ds(pl.multiple_of(g * 8, 8), 8)
        at = g * 512 + half * 16 + row
        heat_in = 0.2 * (rcv[pl.ds(at, 8, stride=64), :] + 1.8)
        cool_in = 0.2 * rcv[pl.ds(at + 32, 8, stride=64), :]
        mass = jnp.zeros((8, 128), F32)
        for c in range(NCAT):
            change = cool_in * rc[c, slots, lanes] - heat_in
            grown = jnp.maximum(thick[c, slots, lanes] + change, 0.0)
            mass = mass + area[c, slots, lanes] * grown
            nt[c, slots, lanes] = pres[c, slots, lanes].astype(F32) * grown
        smass[pl.ds(g * 256 + half * 16 + row, 8, stride=32), :] = mass

    masses = [back(smass, rmass, mass_s, mass_r, i, 0) for i in range(15)]
    for dz in range(4):
        group = (z + 4 - dz) % 4

        @pl.loop(0, 8)
        def _(i):
            for k in range(2):
                for half in range(2):
                    grow(group, i * 2 + k, half)

        for i in range(15):
            if STEPS[i][0] == dz:
                masses[i].start()
    stores = []

    def store(src, dst):
        c = pltpu.make_async_copy(src, dst, osem.at[len(stores)])
        c.start()
        stores.append(c)

    store(nt, nt_hbm)
    rmass[mine, :] = smass[mine, :]
    s1s = [back(ss1, rs1, s1_s, s1_r, i) for i in range(15)]

    at_west, at_east = s == 0, s == 15
    at_south, at_north = r == 0, r == 7
    for c in halo:
        c.wait_recv()

    def beside(right, left, shift_right, shift_left):
        a = jnp.where(at_east, 0.0, pltpu.roll(right, shift_right, 1) if shift_right else right)
        b = jnp.where(at_west, 0.0, pltpu.roll(left, shift_left, 1) if shift_left else left)
        return jnp.where(lane < 16, a, jnp.where(lane >= 112, b, 0.0))

    @pl.loop(0, 36)
    def _(i):
        raw = pl.ds(pl.multiple_of(i * 8, 8), 8)
        at = pl.ds(pl.multiple_of(i * 8 + 8, 8), 8)
        right, left = QR[raw, :], QL[raw, :]
        for f in range(8):
            S[f, 2, at, :] = beside(right, left, (128 - 16 * f) % 128, (112 - 16 * f) % 128)

    def clear_outside(ref, n):
        for at, gone in ((below, at_south), (above, at_north)):
            for f in range(n):
                for t in range(3):
                    ref[f, t, at, :] = jnp.where(gone, 0.0, ref[f, t, at, :])

    clear_outside(S, 8)

    slot_of = []
    for b in range(NBLK):
        slot = owners[b] * 2
        for e in range(b):
            slot = slot + (owners[e] == owners[b]).astype(jnp.int32)
        slot_of.append(slot)
    for c in covs:
        c.wait_recv()
    for k in range(32):
        got[1, k] = rcov[pl.ds(k * 32, 32), :]
    for b in range(NBLK):
        cover = got[1, slot_of[b]]
        damping = jnp.exp(-2.0 * (1.0 - cover))
        temp_b, cool_b = sea[b], air[b]
        for half in range(2):
            part = slice(half * 16, half * 16 + 16)
            lanes = slice(half * 128, half * 128 + 128)
            cv = cover[part]
            M[1, half, pl.ds(OWN + b * 16, 16), :] = damping[part]
            flux[0, half, pl.ds(b * 16, 16), :] = cv * (0.5 * (temp_b[:, lanes] + 1.8)) - (1.0 - cv) * cool_b[:, lanes]
    for c in masses:
        c.wait_recv()
    for k in range(32):
        got[0, k] = rmass[pl.ds(k * 32, 32), :]
    for b in range(NBLK):
        mass = got[0, slot_of[b]]
        for half in range(2):
            rows = pl.ds(OWN + b * 16, 16)
            part = mass[half * 16 : half * 16 + 16]
            M[0, half, rows, :] = part
            M[1, half, rows, :] = M[1, half, rows, :] * part

    for i in range(8):
        left = jnp.zeros((8, 128), F32)
        right = left
        for chunk in range(4):
            for f in range(2):
                at = pl.ds(OWN + chunk * 64 + i * 8, 8)
                k = 32 * chunk + 16 * f
                here = (lane >= k) & (lane < k + 16)
                a, b = M[f, 0, at, :], M[f, 1, at, :]
                left = jnp.where(here, pltpu.roll(a, k, 1) if k else a, left)
                right = jnp.where(here, pltpu.roll(b, (k + 16) % 128, 1) if k != 112 else b, right)
        ML[pl.ds(i * 8, 8), :] = left
        MR[pl.ds(i * 8, 8), :] = right
    sems = (ms, mr)
    halo_m = [
        remote(ML, NR, sems, 0, {"gx": west}),
        remote(MR, NL, sems, 1, {"gx": east}),
        remote(M.at[:, two, first16], M.at[:, two, above], sems, 2, {"gy": south}),
        remote(M.at[:, two, last16], M.at[:, two, below], sems, 3, {"gy": north}),
        remote(ML.at[pl.ds(0, 16)], KR.at[1], sems, 4, {"gy": south, "gx": west}),
        remote(MR.at[pl.ds(0, 16)], KL.at[1], sems, 5, {"gy": south, "gx": east}),
        remote(ML.at[pl.ds(48, 16)], KR.at[0], sems, 6, {"gy": north, "gx": west}),
        remote(MR.at[pl.ds(48, 16)], KL.at[0], sems, 7, {"gy": north, "gx": east}),
    ]
    for c in halo_m:
        c.start()

    def coefficients(t, row0, rows):
        at = pl.ds(row0, rows)
        inertia = M[0, t, at, :] + 0.5
        w = S[WET, t, at, :] / (inertia + 0.24)
        cA[t, at, :] = w * inertia
        cB[t, at, :] = 0.075 * w
        cG[0, t, at, :] = 0.3 * w * S[FU, t, at, :]
        cG[1, t, at, :] = 0.3 * w * S[FV, t, at, :]
        cK[t, at, :] = M[1, t, at, :] * (1.0 / 6.0)

    @pl.loop(0, 4)
    def _(i):
        for t in range(2):
            coefficients(t, pl.multiple_of(OWN + i * 64, 8), 64)

    def across(f, row0, rows, tiles):
        wide = lax.broadcasted_iota(jnp.int32, (rows, 128), 1)
        v = [S[f, t, pl.ds(row0, rows), :] for t in range(3)]
        up = [pltpu.roll(a, 127, 1) for a in v]
        down = [pltpu.roll(a, 1, 1) for a in v]
        return {
            t: jnp.where(wide == 127, up[(t + 1) % 3], up[t]) - jnp.where(wide == 0, down[(t + 2) % 3], down[t])
            for t in tiles
        }

    def along(f, t, row0, rows):
        return S[f, t, pl.ds(row0 + 1, rows), :] - S[f, t, pl.ds(row0 - 1, rows), :]

    def relax(row0, rows, tiles=(0, 1, 2)):
        at = pl.ds(row0, rows)
        ux, vx = across(U, row0, rows, tiles), across(V, row0, rows, tiles)
        for t in tiles:
            a, b = ux[t], along(V, t, row0, rows)
            sh = along(U, t, row0, rows) + vx[t]
            d, e = a + b, a - b
            k = cK[t, at, :]
            d4 = 4.0 * d
            q = d * d4 + e * e + (sh * sh + 0.64)
            f = k * lax.rsqrt(q)
            k2 = k + k
            S[X, t, at, :] = S[X, t, at, :] * (1.0 / 1.5) + (f * (d4 + e) - k2)
            S[Y, t, at, :] = S[Y, t, at, :] * (1.0 / 1.5) + (f * (d4 - e) - k2)
            S[H, t, at, :] = S[H, t, at, :] * (1.0 / 1.5) + (f + f) * sh

    def move(row0, rows, tiles=(0, 1, 2)):
        at = pl.ds(row0, rows)
        xx, hx = across(X, row0, rows, tiles), across(H, row0, rows, tiles)
        for t in tiles:
            a, b = cA[t, at, :], cB[t, at, :]
            fe = xx[t] + along(H, t, row0, rows)
            fn = hx[t] + along(Y, t, row0, rows)
            S[U, t, at, :] = a * S[U, t, at, :] + (b * fe + cG[0, t, at, :])
            S[V, t, at, :] = a * S[V, t, at, :] + (b * fn + cG[1, t, at, :])

    for c in halo:
        c.wait_send()

    @pl.loop(0, 4)
    def _(i):
        relax(pl.multiple_of(OWN + i * 64, 8), 64, (0, 1))

    for c in halo_m:
        c.wait_recv()
    for c in s1s:
        c.start()
    for f in range(2):
        for chunk in range(4):
            k = 32 * chunk + 16 * f
            for i in range(8):
                at = pl.ds(OWN + chunk * 64 + i * 8, 8)
                raw = pl.ds(i * 8, 8)
                M[f, 2, at, :] = beside(NR[raw, :], NL[raw, :], (128 - k) % 128, (112 - k) % 128)
        for i in range(2):
            raw = pl.ds(i * 8, 8)
            k = 96 + 16 * f
            M[f, 2, pl.ds(8 + i * 8, 8), :] = beside(KR[0, raw, :], KL[0, raw, :], 128 - k, (112 - k) % 128)
            k = 16 * f
            M[f, 2, pl.ds(280 + i * 8, 8), :] = beside(KR[1, raw, :], KL[1, raw, :], (128 - k) % 128, 112 - k)
    clear_outside(M, 2)

    for t in range(2):
        coefficients(t, 8, 16)
        coefficients(t, 280, 16)

    @pl.loop(0, 4)
    def _(i):
        coefficients(2, pl.multiple_of(8 + i * 72, 8), 72)

    for t in range(2):
        relax(8, 16, (t,))
        relax(280, 16, (t,))

    @pl.loop(0, 3)
    def _(i):
        relax(pl.multiple_of(8 + i * 96, 8), 96, (2,))

    @pl.loop(1, NSUB)
    def _(n):
        move(8, 288)
        relax(8, 288)

    @pl.loop(0, 4)
    def _(i):
        move(pl.multiple_of(OWN + i * 64, 8), 64, (0, 1))

    @pl.loop(0, 4)
    def _(i):
        at = pl.ds(pl.multiple_of(OWN + i * 64, 8), 64)
        raw = pl.ds(pl.multiple_of(i * 64, 8), 64)
        for t in range(2):
            a, b = S[X, t, at, :], S[Y, t, at, :]
            outb[0, t, raw, :] = 0.5 * (a + b)
            outb[1, t, raw, :] = 0.5 * (a - b)
            outb[2, t, raw, :] = 0.5 * S[H, t, at, :]

    for t in range(2):
        lanes = pl.ds(t * 128, 128)
        store(S.at[pl.ds(U, 2), t, pl.ds(OWN, 256)], velo_hbm.at[:, :, lanes])
        store(outb.at[:, t], stro_hbm.at[:, :, lanes])

    for c in s1s:
        c.wait_recv()
    for k in range(32):
        got[2, k] = rs1[pl.ds(k * 32, 32), :]
    for b in range(NBLK):
        s1, cover = got[2, slot_of[b]], got[1, slot_of[b]]
        temp_b, cool_b = sea[b], air[b]
        for half in range(2):
            part = slice(half * 16, half * 16 + 16)
            lanes = slice(half * 128, half * 128 + 128)
            basal = 0.5 * (temp_b[:, lanes] + 1.8)
            flux[1, half, pl.ds(b * 16, 16), :] = 0.4 * (basal * cover[part] - 0.5 * cool_b[:, lanes] * s1[part])
    for t in range(2):
        store(flux.at[:, t], flux_hbm.at[:, :, pl.ds(t * 128, 128)])
    for c in sends + covs + masses + s1s + halo_m:
        c.wait_send()
    for c in stores:
        c.wait()


def hand_over(nt, flux, velo, stro, nt_out, flux_out, velo_out, stro_out, nt_v, flux_v, velo_v, stro_v, sem):
    parts = [(nt.at[c], nt_v.at[c], nt_out.at[c]) for c in range(NCAT)]
    parts += [(stro.at[c], stro_v.at[c], stro_out.at[c]) for c in range(3)]
    parts += [(velo.at[c], velo_v.at[c], velo_out.at[c]) for c in range(2)]
    parts += [(flux.at[c], flux_v.at[c], flux_out.at[c]) for c in range(2)]
    reads = [pltpu.make_async_copy(a, v, sem.at[0, i]) for i, (a, v, _) in enumerate(parts)]
    writes = [pltpu.make_async_copy(v, b, sem.at[1, i]) for i, (_, v, b) in enumerate(parts)]
    for c in reads:
        c.start()
    for c, d in zip(reads, writes):
        c.wait()
        d.start()
    for d in writes:
        d.wait()


def local(sea, air, cur, wind, land, vel, stress, owner, thick, area, pres):
    any_ = pl.BlockSpec(memory_space=pl.ANY)
    vm = lambda *shape, dtype=F32: pltpu.VMEM(shape, dtype)
    dma = lambda n: pltpu.SemaphoreType.DMA((n,))
    results = (
        jax.ShapeDtypeStruct((NCAT, 32, 4096), F32),
        jax.ShapeDtypeStruct((2, 256, 256), F32),
        jax.ShapeDtypeStruct((2, 256, 256), F32),
        jax.ShapeDtypeStruct((3, 256, 256), F32),
    )
    made = pl.pallas_call(
        kernel,
        out_shape=results,
        in_specs=[pl.BlockSpec(memory_space=pltpu.SMEM)] + [any_] * 10,
        out_specs=(any_,) * 4,
        scratch_shapes=[
            vm(16, 16, 256), vm(16, 16, 256),
            vm(NCAT, 32, 4096), vm(NCAT, 32, 4096), vm(NCAT, 32, 4096, dtype=jnp.int32),
            vm(NCAT, 32, 4096), vm(NCAT, 32, 4096),
            vm(2, 2, 256, 128), vm(2, 2, 256, 128), vm(2, 256, 128, dtype=jnp.int32),
            vm(15 * 128, 128), vm(16 * 128, 128),
            vm(1024, 128), vm(1024, 128), vm(1024, 128),
            vm(1024, 128), vm(1024, 128), vm(1024, 128), vm(3, 32, 32, 128),
            vm(8, 3, ROWS, 128), vm(2, 3, ROWS, 128),
            vm(256, 128), vm(256, 128), vm(288, 128), vm(288, 128),
            vm(64, 128), vm(64, 128), vm(64, 128), vm(64, 128), vm(2, 16, 128), vm(2, 16, 128),
            vm(2, 2, 256, 128),
            vm(3, ROWS, 128), vm(3, ROWS, 128), vm(2, 3, ROWS, 128), vm(3, ROWS, 128),
            vm(3, 2, 256, 128),
            dma(15), dma(10),
            dma(15), dma(15), dma(15), dma(15), dma(15), dma(15), dma(15), dma(15),
            dma(8), dma(8), dma(8), dma(8),
        ],
        compiler_params=pltpu.CompilerParams(
            collective_id=0, has_side_effects=True, vmem_limit_bytes=60 * 1024 * 1024
        ),
    )(
        owner, sea.reshape(16, 16, 256), air.reshape(16, 16, 256), cur, wind, land, vel, stress,
        thick.reshape(NCAT, 32, 4096), area.reshape(NCAT, 32, 4096), pres.reshape(NCAT, 32, 4096),
    )
    nt, flux, velo, stro = pl.pallas_call(
        hand_over,
        out_shape=results,
        in_specs=[any_] * 4,
        out_specs=(any_,) * 4,
        scratch_shapes=[vm(*o.shape) for o in results] + [pltpu.SemaphoreType.DMA((2, 12))],
        compiler_params=pltpu.CompilerParams(vmem_limit_bytes=60 * 1024 * 1024),
    )(*made)
    return nt.reshape(NCAT, 1, 32, 4096), flux, velo, stro


def solution(mesh):
    grid, pair, ice = P("gy", "gx"), P(None, "gy", "gx"), P(None, "gy", "gx", None)
    return jax.shard_map(
        local,
        mesh=mesh,
        in_specs=(grid, grid, pair, pair, grid, pair, pair, grid, ice, ice, ice),
        out_specs=(ice, pair, pair, pair),
        check_vma=False,
    )
```
